512 devices in a mesh: tm: 64 (over z, x), chan: 8 (over y, core).
Axes of the slice: x: 4, y: 4, z: 16, core: 2. Of those that a mesh axis runs over, the one named last changes fastest.
Arguments:
- observations: bfloat16 [8, 512, 4096], P(None, 'tm', 'chan'), may hold values from -6 to 6
- obs_matrix: bfloat16 [4096, 512], P('chan'), may hold values from -0.125 to 0.125
- block_pattern: int32 [32, 4], P('chan'), may hold values 0 or 1
- noise_precision: float32 [4096], P('chan'), may hold values from 0.25 to 4
- retention: float32 [8, 512], replicated, may hold values from 0.25 to 1
- prior_mean: float32 [512], replicated, may hold values from -6 to 6
- filter_matrix: float32 [512, 512], replicated, may hold values from -1 to 1, as said below
- filter_gain: float32 [512, 512], replicated, may hold values from -0.0234375 to 0.0234375
- transition: float32 [512, 512], replicated, may hold values from -0.25 to 0.25
- smoother_gain: float32 [512, 512], replicated, may hold values from -1 to 1, as said below
Outputs:
- filtered: float32 [8, 512, 512], P(None, 'tm', 'chan')
- smoothed: float32 [8, 512, 512], P(None, 'tm', 'chan')
The draws below stay inside these ranges and needn't reach their ends.
Inputs may be any that keep to these rules, and one draw needn't show every extreme that they name: `filter_matrix`: spectral norm below 1. `smoother_gain`: spectral norm below 1.
All inputs are finite; a program needn't handle non-finite values. No bound on the sum of `block_pattern` on one device may be relied on, other than what follows from the above.
Results may differ from the reference program's by a relative error of at most 0.0027.
Values sent between devices are 32-bit elements; how exact they have to be, the bound alone decides.
A program may use at most 64 MiB of HBM per device.

```python
import math
import jax
import jax.numpy as jnp
from jax import lax

S = 512
CH = 4096
BLOCK = 128
TRACK_TOTAL = 8
TIMES = 512


def mixed_matrix(key, slow_share):
    key_flag, key_slow, key_fast, key_dirs = jax.random.split(key, 4)
    slow_flag = jax.random.uniform(key_flag, (S,)) < slow_share
    slow_rate = jax.random.uniform(key_slow, (S,), minval=0.1, maxval=0.5) / TIMES
    fast_rate = jax.random.uniform(key_fast, (S,), minval=1.0 / 50.0, maxval=1.0 / 30.0)
    decay_rate = jnp.where(slow_flag, slow_rate, fast_rate)
    matrix = jnp.diag(jnp.exp(-decay_rate)).astype(jnp.float32)
    normals = jax.random.normal(key_dirs, (24, S), jnp.float32)
    for index in range(24):
        direction = normals[index] / jnp.sqrt(jnp.sum(normals[index] * normals[index]))
        matrix = matrix - 2.0 * jnp.outer(direction, direction @ matrix)
        matrix = matrix - 2.0 * jnp.outer(matrix @ direction, direction)
    return matrix


def draw_filter_matrix(key, part):
    key = jax.random.fold_in(key, 11)
    share = 0.5
    return mixed_matrix(key, share)


def draw_smoother_gain(key, part):
    key = jax.random.fold_in(key, 23)
    share = 0.5
    return mixed_matrix(key, share)


def draw_retention(key, part):
    key = jax.random.fold_in(key, 37)
    random_initial_draw, random_location_choice, random_clustered_lines = jax.random.split(key, 3)
    top_loss = 0.5
    base = 1.0 - jax.random.uniform(random_initial_draw, (TRACK_TOTAL, TIMES), minval=0.0, maxval=top_loss) / TIMES
    spots = jax.random.randint(random_location_choice, (TRACK_TOTAL, 2), 0, TIMES)
    clustered_lines = jax.random.uniform(random_clustered_lines, (TRACK_TOTAL, 2), minval=0.5, maxval=0.8)
    removed_indicator = jnp.arange(TIMES)[None, None, :] == spots[:, :, None]
    magnitude_multiplier = jnp.prod(jnp.where(removed_indicator, clustered_lines[:, :, None], 1.0), axis=1)
    return (base * magnitude_multiplier).astype(jnp.float32)


def plant(result, key, low, largest):
    place = [jax.random.randint(jax.random.fold_in(key, axis), (), 0, length) for axis, length in enumerate(result.shape)]
    longest = result.shape.index(max(result.shape))
    neighbour = place[:longest] + [(place[longest] + 1) % result.shape[longest]] + place[longest + 1:]
    return result.at[tuple(place)].set(low).at[tuple(neighbour)].set(largest)


def steps_of(stream_key, shape, pieces, smallest, high):
    loudness, own = 1.0, jax.random.fold_in(stream_key, 6)
    for axis_at, parts in pieces:
        heights = jnp.exp(jax.random.uniform(jax.random.fold_in(own, axis_at), (parts,), jnp.float32, smallest / len(pieces), high / len(pieces)))
        loudness = loudness * jnp.repeat(heights, shape[axis_at] // parts).reshape([-1 if axis == axis_at else 1 for axis in range(len(shape))])
    return loudness


def bell_draw(rng, shape, deviation, bound, pieces=(), held_as=jnp.bfloat16):
    loudness = steps_of(rng, shape, pieces, -0.22, 0.18) if pieces else 1.0
    values = jax.random.normal(rng, shape, jnp.float32) * deviation * loudness
    return jnp.minimum(jnp.maximum(values, -bound), bound).astype(held_as)


def setup_inputs(seed: int = 0) -> dict:
    streams_of = jax.random.split(jax.random.key(seed), 11)
    observations = bell_draw(streams_of[0], (TRACK_TOTAL, TIMES, CH), 1.0, 6.0, ((1, 64), (2, 8)))
    obs_matrix = bell_draw(streams_of[1], (CH, S), (CH // 2) ** -0.5, 0.125, ((0, 8),))
    block_pattern = plant((jax.random.randint(streams_of[2], (CH // BLOCK, S // BLOCK), 0, 2) < 1).astype(jnp.int32), jax.random.fold_in(streams_of[2], 1), 0, 1)
    noise_precision = jnp.clip(jnp.exp(math.log(4.0) - 2.7725887 * jax.random.uniform(streams_of[3], (CH,), jnp.float32) ** steps_of(streams_of[3], (CH,), ((0, 8),), -0.2, 0.2)), 0.25, 4.0)
    retention = draw_retention(jax.random.fold_in(streams_of[10], 71), 0)
    prior_mean = bell_draw(streams_of[5], (S,), 1.0, 6.0, (), jnp.float32)
    filter_matrix = draw_filter_matrix(jax.random.fold_in(streams_of[10], 71), 0)
    filter_gain = bell_draw(streams_of[7], (S, S), (S * TIMES // 4) ** -0.5, 0.0234375, (), jnp.float32)
    transition = bell_draw(streams_of[8], (S, S), S ** -0.5, 0.25, (), jnp.float32)
    smoother_gain = draw_smoother_gain(jax.random.fold_in(streams_of[10], 71), 0)
    return dict(observations=observations, obs_matrix=obs_matrix, block_pattern=block_pattern, noise_precision=noise_precision, retention=retention, prior_mean=prior_mean, filter_matrix=filter_matrix, filter_gain=filter_gain, transition=transition, smoother_gain=smoother_gain)


def reference(observations, obs_matrix, block_pattern, noise_precision, retention, prior_mean, filter_matrix, filter_gain, transition, smoother_gain):
    highest = lax.Precision.HIGHEST
    block_mask = jnp.repeat(jnp.repeat(block_pattern, BLOCK, axis=0), BLOCK, axis=1).astype(jnp.bfloat16)
    obs_used = obs_matrix * block_mask
    weighted = (observations.astype(jnp.float32) * noise_precision).astype(jnp.bfloat16)
    information = jnp.dot(weighted.reshape(TRACK_TOTAL * TIMES, CH), obs_used, preferred_element_type=jnp.float32)
    driving = jnp.dot(information, filter_gain, precision=highest, preferred_element_type=jnp.float32)
    driving = driving.reshape(TRACK_TOTAL, TIMES, S)

    def advance(state, inputs):
        retain_now, forcing = inputs
        state = retain_now[:, None] * jnp.dot(state, filter_matrix, precision=highest, preferred_element_type=jnp.float32) + forcing
        return state, state

    opening_state = jnp.broadcast_to(prior_mean, (TRACK_TOTAL, S)).astype(jnp.float32)
    _, filter_states = lax.scan(advance, opening_state, (jnp.swapaxes(retention, 0, 1), jnp.swapaxes(driving, 0, 1)))
    filtered = jnp.swapaxes(filter_states, 0, 1)
    predicted = jnp.dot(filtered.reshape(TRACK_TOTAL * TIMES, S), transition, precision=highest, preferred_element_type=jnp.float32)
    correction = filtered - jnp.dot(predicted, smoother_gain, precision=highest, preferred_element_type=jnp.float32).reshape(TRACK_TOTAL, TIMES, S)
    boundary = predicted.reshape(TRACK_TOTAL, TIMES, S)[:, TIMES - 1, :]

    def retreat(state, forcing):
        state = jnp.dot(state, smoother_gain, precision=highest, preferred_element_type=jnp.float32) + forcing
        return state, state

    _, smooth_states = lax.scan(retreat, boundary, jnp.swapaxes(correction, 0, 1), reverse=True)
    smoothed = jnp.swapaxes(smooth_states, 0, 1)
    return filtered, smoothed
```

```python
import functools

import jax
import jax.numpy as jnp
from jax import lax
from jax.experimental import pallas as pl
from jax.experimental.pallas import tpu as pltpu
from jax.sharding import PartitionSpec as P

BLOCK = 128
PLANE = 4
MESH = pl.DeviceIdType.MESH
f32 = jnp.float32
bf16 = jnp.bfloat16


def dot(a, b):
    return jnp.dot(a, b, preferred_element_type=f32)


def split(x):
    high = x.astype(bf16)
    return high, (x - high.astype(f32)).astype(bf16)


def times(x, high, low):
    rows = x.shape[0]
    if rows % 16:
        x_high = x.astype(bf16).astype(f32)
        both = jnp.concatenate([x_high, x - x_high], 0).astype(bf16)
        first, second = dot(both, high), dot(both, low)
        return first[:rows] + (first[rows:] + second[:rows])
    x_high, x_low = split(x)
    if rows >= 256:
        return dot(x_high, high) + (dot(x_low, high) + dot(x_high, low))
    first = dot(jnp.concatenate([x_high, x_low], 0), high)
    return first[:rows] + (first[rows:] + dot(x_high, low))


def shifted(x, distance):
    return jnp.roll(x, distance, axis=0)


def kernel(
    nx, nz, nc, steps, width, channels,
    obs_hbm, mat_hbm, pattern, noise, retention, prior, f_hbm, k_hbm, t_hbm, g_hbm,
    filtered, smoothed,
    obs, mat, raw, fh, fl, gh, gl, wh, wl, kh, kl,
    part, part_in, drive, ends, starts, rho, rows_y, rows_c, fbuf, cbuf, bbuf,
    out_f, out_s, in_f, in_s,
    load_sem, rs_send, rs_recv, x_send, x_recv, e_send, e_recv, b_send, b_recv,
    of_send, of_recv, os_send, os_recv,
):
    tm, chan = lax.axis_index("tm"), lax.axis_index("chan")
    z, x = tm // nx, tm % nx
    span = nx * steps
    total = nz * span
    local_bits = span.bit_length() - 1
    z_bits = nz.bit_length() - 1

    loads = [
        pltpu.make_async_copy(source, target, load_sem.at[i])
        for i, (source, target) in enumerate(
            (
                (mat_hbm, mat),
                (obs_hbm, obs),
                (f_hbm, raw.at[0]),
                (k_hbm, raw.at[1]),
                (g_hbm, raw.at[2]),
                (t_hbm, raw.at[3]),
            )
        )
    ]
    for load in loads:
        load.start()

    def chan_peer(i):
        return {"chan": lax.rem(chan + i, nc)}

    def x_peer(i):
        return {"tm": z * nx + lax.rem(x + i, nx)}

    def z_peer(i):
        return {"tm": lax.rem(z + i, nz) * nx + x}

    barrier = pltpu.get_barrier_semaphore()
    for i in range(1, nz):
        pl.semaphore_signal(barrier, inc=1, device_id=z_peer(i), device_id_type=MESH)
    for i in range(1, nx):
        pl.semaphore_signal(barrier, inc=1, device_id=x_peer(i), device_id_type=MESH)
    for i in range(1, nc):
        pl.semaphore_signal(barrier, inc=1, device_id=chan_peer(i), device_id_type=MESH)

    def remote(source, target, send, recv, peer):
        return pltpu.make_async_remote_copy(
            src_ref=source, dst_ref=target, send_sem=send, recv_sem=recv,
            device_id=peer, device_id_type=MESH,
        )

    def square(high, low, first, last):
        def body(i, _):
            a, b = high[i], low[i]
            h, l = split(dot(a, a) + (dot(a, b) + dot(b, a)))
            high[i + 1] = h
            low[i + 1] = l
            return 0

        lax.fori_loop(first, last, body, 0)

    loads[0].wait()
    loads[1].wait()
    weighted = obs[...].astype(f32) * noise[...].reshape(1, 1, channels)
    weighted = weighted.reshape(nc * steps, channels).astype(bf16)
    lane_block = lax.broadcasted_iota(jnp.int32, (BLOCK, width), 1) // BLOCK
    used = []
    for i in range(channels // BLOCK):
        mask = jnp.zeros((BLOCK, width), f32)
        for j in range(width // BLOCK):
            mask = jnp.where(lane_block == j, pattern[i, j].astype(f32), mask)
        used.append(mat[i * BLOCK : (i + 1) * BLOCK] * mask.astype(bf16))
    part[...] = dot(weighted, jnp.concatenate(used, 0)).reshape(nc, steps, width)

    loads[2].wait()
    fh[0], fl[0] = split(raw[0])
    square(fh, fl, 0, 2)

    pl.semaphore_wait(barrier, nz + nx + nc - 3)
    sums = []
    for i in range(1, nc):
        there = lax.rem(chan + i, nc)
        copy = remote(part.at[there], part_in.at[chan], rs_send.at[i], rs_recv.at[i], chan_peer(i))
        copy.start()
        sums.append(copy)
    part_in[chan] = part[chan]

    row = retention[pl.ds(chan, 1), :]
    here = lax.broadcasted_iota(jnp.int32, (total, total), 0)
    there = lax.broadcasted_iota(jnp.int32, (total, total), 1)
    picked = jnp.where(there == (here % nz) * span + here // nz, row, 0.0)
    column = jnp.sum(picked, axis=1, keepdims=True)
    running = column[:nz]
    rho[:nz] = running
    for t in range(1, span):
        running = running * column[t * nz : (t + 1) * nz]
        rho[t * nz : (t + 1) * nz] = running
    block_row = lax.broadcasted_iota(jnp.int32, (nz, 1), 0)
    chain = jnp.where(block_row >= 1, shifted(running, 1), 0.0)
    block_factors = [chain]
    for level in range(1, z_bits):
        chain = chain * shifted(chain, 1 << (level - 1))
        block_factors.append(jnp.where(block_row >= (1 << level), chain, 0.0))
    step_row = lax.broadcasted_iota(jnp.int32, (span, 1), 0)
    here = lax.broadcasted_iota(jnp.int32, (span, total), 0)
    there = lax.broadcasted_iota(jnp.int32, (span, total), 1)
    own = jnp.sum(jnp.where(there == here + z * span, row, 0.0), axis=1, keepdims=True)
    own_factors = [jnp.where(step_row >= 1, own, 0.0)]
    for level in range(1, local_bits):
        own = own * shifted(own, 1 << (level - 1))
        own_factors.append(jnp.where(step_row >= (1 << level), own, 0.0))

    loads[3].wait()
    kh[...], kl[...] = split(raw[1])
    square(fh, fl, 2, local_bits)

    for copy in sums:
        copy.wait()
    information = part_in[0]
    for i in range(1, nc):
        information = information + part_in[i]
    drive[x] = times(information, kh[...], kl[...])
    spread = []
    for i in range(1, nx):
        copy = remote(drive.at[x], drive.at[x], x_send.at[i], x_recv.at[i], x_peer(i))
        copy.start()
        spread.append(copy)

    loads[4].wait()
    loads[5].wait()
    gh[0], gl[0] = split(raw[2])
    th, tl = split(raw[3])
    eye = lax.broadcasted_iota(jnp.int32, (width, width), 0) == lax.broadcasted_iota(
        jnp.int32, (width, width), 1
    )
    product = dot(th, gh[0]) + (dot(th, gl[0]) + dot(tl, gh[0]))
    wh[...], wl[...] = split(jnp.where(eye, 1.0, 0.0) - product)
    square(gh, gl, 0, 3)

    for copy in spread:
        copy.wait()

    local = drive[...].reshape(span, width)
    for level in range(local_bits):
        moved = shifted(local, 1 << level)
        local = local + own_factors[level] * times(moved, fh[level], fl[level])
    ends[z] = local[span - 1 :]
    across = []
    for i in sorted(range(1, nz), key=lambda i: -min(i, nz - i)):
        copy = remote(ends.at[z], ends.at[z], e_send.at[i], e_recv.at[i], z_peer(i))
        copy.start()
        across.append(copy)

    square(gh, gl, 3, 4)
    last_plane = z == nz - 1
    corrected = times(local, wh[...], wl[...])
    corrected = jnp.where(last_plane & (step_row == span - 1), local, corrected)
    backward = corrected
    for level in (2, 1, 0):
        backward = backward + times(shifted(backward, -(1 << level)), gh[level], gl[level])
    bbuf[...] = backward.reshape(nx, steps, width)
    for level in range(local_bits - 1, 2, -1):
        backward = backward + times(shifted(backward, -(1 << level)), gh[level], gl[level])
    starts[z] = backward[:1]
    for i in sorted(range(1, nz), key=lambda i: -min(i, nz - i)):
        copy = remote(starts.at[z], starts.at[z], b_send.at[i], b_recv.at[i], z_peer(i))
        copy.start()
        across.append(copy)

    square(fh, fl, local_bits, local_bits + z_bits - 1)
    square(gh, gl, 4, local_bits + z_bits - 1)

    for copy in across[: nz - 1]:
        copy.wait()

    carry = jnp.where(block_row == 0, prior[...], shifted(ends[...].reshape(nz, width), 1))
    for level in range(z_bits):
        moved = shifted(carry, 1 << level)
        high, low = fh[local_bits + level], fl[local_bits + level]
        carry = carry + block_factors[level] * times(moved, high, low)

    rows_y[:nz] = times(carry, fh[0], fl[0])
    for level in range(local_bits):
        count = nz << level
        rows_y[count : 2 * count] = times(rows_y[:count], fh[level], fl[level])
    scaled = rows_y[...] * rho[...]
    is_own = lax.broadcasted_iota(jnp.int32, (1, nz, 1), 1) == z
    picked = jnp.sum(jnp.where(is_own, scaled.reshape(span, nz, width), 0.0), axis=1)
    fbuf[...] = (local + picked).reshape(nx, steps, width)

    def send_out(state, out, into, send, recv):
        copies = []
        for k in range(width // BLOCK):
            out[k] = state[:, k * BLOCK : (k + 1) * BLOCK]
        for i in range(1, nc):
            there = lax.rem(chan + i, nc)
            copy = remote(out.at[there // 2], into.at[chan], send.at[i], recv.at[i], chan_peer(i))
            copy.start()
            copies.append(copy)
        into[chan] = out[chan // 2]
        return copies

    copies_f = send_out(fbuf[x], out_f, in_f, of_send, of_recv)

    turned = times(rows_y[...] * rho[...], wh[...], wl[...])
    final = lax.broadcasted_iota(jnp.int32, (total, 1), 0) == total - 1
    turned = jnp.where(final, rows_y[...] * rho[...], turned)
    rows_c[...] = turned.reshape(nx, steps, nz, width)
    for t in range(span):
        row = rows_c[t // steps, t % steps]
        row = jnp.sum(jnp.where(block_row == z, row, 0.0), axis=0, keepdims=True)
        cbuf[t // steps, t % steps : t % steps + 1] = row
    cbuf[...] = cbuf[...] + corrected.reshape(nx, steps, width)

    for level in (2, 1, 0):
        half = 1 << level
        few = max(1, min(nx, 128 // (half * nz)))

        def reduce_rows(i, _):
            q = pl.ds(i * few, few)
            upper = rows_c[q, half : 2 * half].reshape(few * half * nz, width)
            upper = times(upper, gh[level], gl[level]).reshape(few, half, nz, width)
            rows_c[q, :half] = rows_c[q, :half] + upper
            return 0

        lax.fori_loop(0, nx // few, reduce_rows, 0)

    for copy in across[nz - 1 :]:
        copy.wait()
    whole = block_row == z
    for q in range(nx):
        own_start = bbuf[q][:1]
        if q == 0:
            extra = jnp.where(whole, own_start, starts[...].reshape(nz, width))
        else:
            extra = jnp.where(whole, own_start, 0.0)
        value = rows_c[q, 0] + extra
        rows_y[q * nz : (q + 1) * nz] = value
        later = jnp.where(block_row < nz - 1, shifted(value, -1), 0.0)
        rows_y[(nx + q) * nz : (nx + q + 1) * nz] = later
    first = pl.multiple_of((1 + x) * nz, nz)
    tail = rows_y[pl.ds(first, nx * nz), :]
    for level in range(local_bits - 1, 2, -1):
        half = nz << (level - 3)
        tail = tail[:half] + times(tail[half:], gh[level], gl[level])
    for level in range(z_bits):
        distance = 1 << level
        moved = jnp.where(block_row < nz - distance, shifted(tail, -distance), 0.0)
        high, low = gh[local_bits + level], gl[local_bits + level]
        tail = tail + times(moved, high, low)
    after = jnp.sum(jnp.where(whole, tail, 0.0), axis=0, keepdims=True)

    row8 = lax.broadcasted_iota(jnp.int32, (steps, 1), 0)
    placed = jnp.where(row8 == steps - 1, after, 0.0)
    state = cbuf[x] + times(placed, gh[0], gl[0])
    for level in range(3):
        distance = 1 << level
        moved = jnp.where(row8 < steps - distance, shifted(state, -distance), 0.0)
        state = state + times(moved, gh[level], gl[level])
    copies_s = send_out(state, out_s, in_s, os_send, os_recv)

    odd = lax.rem(chan, 2) == 1
    half = BLOCK // 2
    for copies, into, result in ((copies_f, in_f, filtered), (copies_s, in_s, smoothed)):
        for copy in copies:
            copy.wait()
        both = into[...]
        result[...] = jnp.where(odd, both[:, :, half:], both[:, :, :half])


def build(mesh, nx):
    nc = mesh.shape["chan"]
    nz = mesh.shape["tm"] // nx

    def per_device(
        observations, obs_matrix, block_pattern, noise_precision, retention, prior_mean,
        filter_matrix, filter_gain, transition, smoother_gain,
    ):
        series, steps, channels = observations.shape
        width = obs_matrix.shape[1]
        span = nx * steps
        total = span * nz
        powers = total.bit_length() - 1
        vmem = pl.BlockSpec(memory_space=pltpu.VMEM)
        smem = pl.BlockSpec(memory_space=pltpu.SMEM)
        hbm = pl.BlockSpec(memory_space=pl.ANY)
        dma = pltpu.SemaphoreType.DMA
        square = (width, width)
        blocks = width // BLOCK
        result = jax.ShapeDtypeStruct((series, steps, width // nc), f32)
        return pl.pallas_call(
            functools.partial(kernel, nx, nz, nc, steps, width, channels),
            out_shape=(result, result),
            in_specs=[hbm, hbm, smem, vmem, vmem, vmem, hbm, hbm, hbm, hbm],
            out_specs=(vmem, vmem),
            scratch_shapes=[
                pltpu.VMEM((series, steps, channels), bf16),
                pltpu.VMEM((channels, width), bf16),
                pltpu.VMEM((4, *square), f32),
                pltpu.VMEM((powers, *square), bf16),
                pltpu.VMEM((powers, *square), bf16),
                pltpu.VMEM((powers, *square), bf16),
                pltpu.VMEM((powers, *square), bf16),
                pltpu.VMEM(square, bf16),
                pltpu.VMEM(square, bf16),
                pltpu.VMEM(square, bf16),
                pltpu.VMEM(square, bf16),
                pltpu.VMEM((nc, steps, width), f32),
                pltpu.VMEM((nc, steps, width), f32),
                pltpu.VMEM((nx, steps, width), f32),
                pltpu.VMEM((nz, 1, width), f32),
                pltpu.VMEM((nz, 1, width), f32),
                pltpu.VMEM((total, 1), f32),
                pltpu.VMEM((total, width), f32),
                pltpu.VMEM((nx, steps, nz, width), f32),
                pltpu.VMEM((nx, steps, width), f32),
                pltpu.VMEM((nx, steps, width), f32),
                pltpu.VMEM((nx, steps, width), f32),
                pltpu.VMEM((blocks, steps, BLOCK), f32),
                pltpu.VMEM((blocks, steps, BLOCK), f32),
                pltpu.VMEM((nc, steps, BLOCK), f32),
                pltpu.VMEM((nc, steps, BLOCK), f32),
                dma((6,)),
                dma((nc,)), dma((nc,)),
                dma((nx,)), dma((nx,)),
                dma((nz,)), dma((nz,)),
                dma((nz,)), dma((nz,)),
                dma((nc,)), dma((nc,)),
                dma((nc,)), dma((nc,)),
            ],
            compiler_params=pltpu.CompilerParams(
                collective_id=0, has_side_effects=True, vmem_limit_bytes=48 * 1024 * 1024
            ),
        )(
            observations, obs_matrix, block_pattern, noise_precision.reshape(1, channels),
            retention, prior_mean.reshape(1, width),
            filter_matrix, filter_gain, transition, smoother_gain,
        )

    placed = (
        P(None, "tm", "chan"), P("chan", None), P("chan", None), P("chan"),
        P(), P(), P(), P(), P(), P(),
    )
    return jax.shard_map(
        per_device,
        mesh=mesh,
        in_specs=placed,
        out_specs=(P(None, "tm", "chan"), P(None, "tm", "chan")),
        check_vma=False,
    )


def solution(mesh):
    return build(mesh, PLANE)
```

```python
import functools

import jax
import jax.numpy as jnp
from jax import lax
from jax.experimental import pallas as pl
from jax.experimental.pallas import tpu as pltpu
from jax.sharding import PartitionSpec as P

BLOCK = 128
PLANE = 4
LIMIT = 63 * 1024 * 1024
MESH = pl.DeviceIdType.MESH
f32 = jnp.float32
bf16 = jnp.bfloat16


def dot(a, b):
    return jnp.dot(a, b, preferred_element_type=f32)


def split(x):
    high = x.astype(bf16)
    return high, (x - high.astype(f32)).astype(bf16)


def times(x, high, low):
    rows = x.shape[0]
    if rows % 16:
        x_high = x.astype(bf16).astype(f32)
        both = jnp.concatenate([x_high, x - x_high], 0).astype(bf16)
        first, second = dot(both, high), dot(both, low)
        return first[:rows] + (first[rows:] + second[:rows])
    x_high, x_low = split(x)
    if rows >= 256:
        return dot(x_high, high) + (dot(x_low, high) + dot(x_high, low))
    first = dot(jnp.concatenate([x_high, x_low], 0), high)
    return first[:rows] + (first[rows:] + dot(x_high, low))


def shifted(x, distance):
    return jnp.roll(x, distance, axis=0)


def kernel(
    nx, nz, nc, steps, width, channels,
    obs_hbm, mat_hbm, pattern_hbm, noise_hbm, retention_hbm, prior_hbm, f_hbm, k_hbm, t_hbm, g_hbm,
    filtered, smoothed,
    obs, mat, pattern, noise, retention, prior, raw, fh, fl, gh, gl, wh, wl, kh, kl,
    part, part_in, drive, ends, starts, rho, rows_y, rows_c, fbuf, cbuf, bbuf,
    out_f, out_s, in_f, in_s,
    load_sem, rs_send, rs_recv, x_send, x_recv, e_send, e_recv, b_send, b_recv,
    of_send, of_recv, os_send, os_recv,
):
    tm, chan = lax.axis_index("tm"), lax.axis_index("chan")
    z, x = tm // nx, tm % nx
    span = nx * steps
    total = nz * span
    local_bits = span.bit_length() - 1
    z_bits = nz.bit_length() - 1

    loads = [
        pltpu.make_async_copy(source, target, load_sem.at[i])
        for i, (source, target) in enumerate(
            (
                (obs_hbm, obs),
                (mat_hbm, mat),
                (pattern_hbm, pattern),
                (noise_hbm, noise),
                (f_hbm, raw.at[0]),
                (k_hbm, raw.at[1]),
                (g_hbm, raw.at[2]),
                (t_hbm, raw.at[3]),
                (retention_hbm, retention),
                (prior_hbm, prior),
            )
        )
    ]
    for load in loads:
        load.start()

    def chan_peer(i):
        return {"chan": lax.rem(chan + i, nc)}

    def x_peer(i):
        return {"tm": z * nx + lax.rem(x + i, nx)}

    def z_peer(i):
        return {"tm": lax.rem(z + i, nz) * nx + x}

    barrier = pltpu.get_barrier_semaphore()
    for i in range(1, nz):
        pl.semaphore_signal(barrier, inc=1, device_id=z_peer(i), device_id_type=MESH)
    for i in range(1, nx):
        pl.semaphore_signal(barrier, inc=1, device_id=x_peer(i), device_id_type=MESH)
    for i in range(1, nc):
        pl.semaphore_signal(barrier, inc=1, device_id=chan_peer(i), device_id_type=MESH)

    def remote(source, target, send, recv, peer):
        return pltpu.make_async_remote_copy(
            src_ref=source, dst_ref=target, send_sem=send, recv_sem=recv,
            device_id=peer, device_id_type=MESH,
        )

    def square(high, low, first, last):
        def body(i, _):
            a, b = high[i], low[i]
            h, l = split(dot(a, a) + (dot(a, b) + dot(b, a)))
            high[i + 1] = h
            low[i + 1] = l
            return 0

        lax.fori_loop(first, last, body, 0)

    for load in loads[:4]:
        load.wait()
    weighted = obs[...].astype(f32) * noise[...].reshape(1, 1, channels)
    weighted = weighted.reshape(nc * steps, channels).astype(bf16)
    lane_block = lax.broadcasted_iota(jnp.int32, (BLOCK, width), 1) // BLOCK
    used = []
    for i in range(channels // BLOCK):
        mask = jnp.zeros((BLOCK, width), f32)
        for j in range(width // BLOCK):
            mask = jnp.where(lane_block == j, pattern[i, j].astype(f32), mask)
        used.append(mat[i * BLOCK : (i + 1) * BLOCK] * mask.astype(bf16))
    part[...] = dot(weighted, jnp.concatenate(used, 0)).reshape(nc, steps, width)

    loads[4].wait()
    fh[0], fl[0] = split(raw[0])
    square(fh, fl, 0, 2)

    pl.semaphore_wait(barrier, nz + nx + nc - 3)
    sums = []
    for i in range(1, nc):
        there = lax.rem(chan + i, nc)
        copy = remote(part.at[there], part_in.at[chan], rs_send.at[i], rs_recv.at[i], chan_peer(i))
        copy.start()
        sums.append(copy)
    part_in[chan] = part[chan]

    loads[8].wait()
    loads[9].wait()
    row = retention[pl.ds(chan, 1), :]
    index = lax.broadcasted_iota(jnp.int32, (total, 1), 0)
    plane, rest = index % nz, index // nz
    wanted = plane * span + (rest % nx) * steps + rest // nx
    there = lax.broadcasted_iota(jnp.int32, (total, total), 1)
    column = jnp.sum(jnp.where(there == wanted, row, 0.0), axis=1, keepdims=True)

    def rows_of(t):
        start = ((t % steps) * nx + t // steps) * nz
        return slice(start, start + nz)

    running = column[:nz]
    rho[:nz] = running
    for t in range(1, span):
        running = running * column[rows_of(t)]
        rho[rows_of(t)] = running
    block_row = lax.broadcasted_iota(jnp.int32, (nz, 1), 0)
    chain = jnp.where(block_row >= 1, shifted(running, 1), 0.0)
    block_factors = [chain]
    for level in range(1, z_bits):
        chain = chain * shifted(chain, 1 << (level - 1))
        block_factors.append(jnp.where(block_row >= (1 << level), chain, 0.0))
    step_row = lax.broadcasted_iota(jnp.int32, (span, 1), 0)
    here = lax.broadcasted_iota(jnp.int32, (span, total), 0)
    there = lax.broadcasted_iota(jnp.int32, (span, total), 1)
    own = jnp.sum(jnp.where(there == here + z * span, row, 0.0), axis=1, keepdims=True)
    own_factors = [jnp.where(step_row >= 1, own, 0.0)]
    for level in range(1, local_bits):
        own = own * shifted(own, 1 << (level - 1))
        own_factors.append(jnp.where(step_row >= (1 << level), own, 0.0))

    loads[5].wait()
    kh[...], kl[...] = split(raw[1])
    square(fh, fl, 2, 4)

    loads[6].wait()
    loads[7].wait()
    gh[0], gl[0] = split(raw[2])
    th, tl = split(raw[3])
    eye = lax.broadcasted_iota(jnp.int32, (width, width), 0) == lax.broadcasted_iota(
        jnp.int32, (width, width), 1
    )
    product = dot(th, gh[0]) + (dot(th, gl[0]) + dot(tl, gh[0]))
    wh[...], wl[...] = split(jnp.where(eye, 1.0, 0.0) - product)

    for copy in sums:
        copy.wait()
    information = part_in[0]
    for i in range(1, nc):
        information = information + part_in[i]
    drive[x] = times(information, kh[...], kl[...])
    spread = []
    for i in range(1, nx):
        copy = remote(drive.at[x], drive.at[x], x_send.at[i], x_recv.at[i], x_peer(i))
        copy.start()
        spread.append(copy)

    square(gh, gl, 0, 3)

    for copy in spread:
        copy.wait()

    local = drive[...].reshape(span, width)
    for level in range(local_bits):
        moved = shifted(local, 1 << level)
        local = local + own_factors[level] * times(moved, fh[level], fl[level])
    ends[z] = local[span - 1 :]
    fbuf[...] = local.reshape(nx, steps, width)
    across = []
    for i in sorted(range(1, nz), key=lambda i: -min(i, nz - i)):
        copy = remote(ends.at[z], ends.at[z], e_send.at[i], e_recv.at[i], z_peer(i))
        copy.start()
        across.append(copy)

    square(gh, gl, 3, 4)
    last_plane = z == nz - 1
    corrected = times(local, wh[...], wl[...])
    corrected = jnp.where(last_plane & (step_row == span - 1), local, corrected)
    cbuf[...] = corrected.reshape(nx, steps, width)
    backward = corrected
    for level in (2, 1, 0):
        backward = backward + times(shifted(backward, -(1 << level)), gh[level], gl[level])
    bbuf[...] = backward.reshape(nx, steps, width)
    for level in range(local_bits - 1, 2, -1):
        backward = backward + times(shifted(backward, -(1 << level)), gh[level], gl[level])
    starts[z] = backward[:1]
    for i in sorted(range(1, nz), key=lambda i: -min(i, nz - i)):
        copy = remote(starts.at[z], starts.at[z], b_send.at[i], b_recv.at[i], z_peer(i))
        copy.start()
        across.append(copy)

    square(fh, fl, 4, local_bits + z_bits - 1)
    square(gh, gl, 4, local_bits + z_bits - 1)

    for copy in across[: nz - 1]:
        copy.wait()

    carry = jnp.where(block_row == 0, prior[...], shifted(ends[...].reshape(nz, width), 1))
    for level in range(z_bits):
        moved = shifted(carry, 1 << level)
        high, low = fh[local_bits + level], fl[local_bits + level]
        carry = carry + block_factors[level] * times(moved, high, low)

    rows_y[:nz] = times(carry, fh[0], fl[0])
    count = nz
    for level in (*range(3, local_bits), 0, 1, 2):
        rows_y[count : 2 * count] = times(rows_y[:count], fh[level], fl[level])
        count = 2 * count
    rows_y[...] = rows_y[...] * rho[...]

    def own_rows(rows):
        return jnp.concatenate([rows[pl.ds((p * nx + x) * nz + z, 1), :] for p in range(steps)], 0)

    def send_out(state, out, into, send, recv):
        copies = []
        for k in range(width // BLOCK):
            out[k] = state[:, k * BLOCK : (k + 1) * BLOCK]
        for i in range(1, nc):
            there = lax.rem(chan + i, nc)
            copy = remote(out.at[there // 2], into.at[chan], send.at[i], recv.at[i], chan_peer(i))
            copy.start()
            copies.append(copy)
        into[chan] = out[chan // 2]
        return copies

    copies_f = send_out(fbuf[x] + own_rows(rows_y), out_f, in_f, of_send, of_recv)

    rows_c[...] = times(rows_y[...], wh[...], wl[...])
    rows_c[total - 1 :] = rows_y[total - 1 :]
    own_corrected = cbuf[x] + own_rows(rows_c)

    for level in (2, 1, 0):
        half = nx * nz << level
        rows_c[:half] = rows_c[:half] + times(rows_c[half : 2 * half], gh[level], gl[level])

    for copy in across[nz - 1 :]:
        copy.wait()
    whole = block_row == z
    for q in range(nx):
        own_start = bbuf[q][:1]
        if q == 0:
            extra = jnp.where(whole, own_start, starts[...].reshape(nz, width))
        else:
            extra = jnp.where(whole, own_start, 0.0)
        value = rows_c[q * nz : (q + 1) * nz] + extra
        rows_y[q * nz : (q + 1) * nz] = value
        later = jnp.where(block_row < nz - 1, shifted(value, -1), 0.0)
        rows_y[(nx + q) * nz : (nx + q + 1) * nz] = later
    first = pl.multiple_of((1 + x) * nz, nz)
    tail = rows_y[pl.ds(first, nx * nz), :]
    for level in range(local_bits - 1, 2, -1):
        half = nz << (level - 3)
        tail = tail[:half] + times(tail[half:], gh[level], gl[level])
    for level in range(z_bits):
        distance = 1 << level
        moved = jnp.where(block_row < nz - distance, shifted(tail, -distance), 0.0)
        high, low = gh[local_bits + level], gl[local_bits + level]
        tail = tail + times(moved, high, low)
    after = jnp.sum(jnp.where(whole, tail, 0.0), axis=0, keepdims=True)

    row8 = lax.broadcasted_iota(jnp.int32, (steps, 1), 0)
    placed = jnp.where(row8 == steps - 1, after, 0.0)
    state = own_corrected + times(placed, gh[0], gl[0])
    for level in range(3):
        distance = 1 << level
        moved = jnp.where(row8 < steps - distance, shifted(state, -distance), 0.0)
        state = state + times(moved, gh[level], gl[level])
    copies_s = send_out(state, out_s, in_s, os_send, os_recv)

    for copies, into, result in ((copies_f, in_f, filtered), (copies_s, in_s, smoothed)):
        for copy in copies:
            copy.wait()
        result[...] = into[...]


def build(mesh, nx):
    nc = mesh.shape["chan"]
    nz = mesh.shape["tm"] // nx

    def per_device(
        observations, obs_matrix, block_pattern, noise_precision, retention, prior_mean,
        filter_matrix, filter_gain, transition, smoother_gain,
    ):
        series, steps, channels = observations.shape
        width = obs_matrix.shape[1]
        span = nx * steps
        total = span * nz
        powers = total.bit_length() - 1
        vmem = pl.BlockSpec(memory_space=pltpu.VMEM)
        hbm = pl.BlockSpec(memory_space=pl.ANY)
        dma = pltpu.SemaphoreType.DMA
        square = (width, width)
        blocks = width // BLOCK
        result = jax.ShapeDtypeStruct((series, steps, BLOCK), f32)
        both = pl.pallas_call(
            functools.partial(kernel, nx, nz, nc, steps, width, channels),
            out_shape=(result, result),
            in_specs=[hbm] * 10,
            out_specs=(vmem, vmem),
            scratch_shapes=[
                pltpu.VMEM((series, steps, channels), bf16),
                pltpu.VMEM((channels, width), bf16),
                pltpu.SMEM((channels // BLOCK, width // BLOCK), jnp.int32),
                pltpu.VMEM((1, channels), f32),
                pltpu.VMEM((series, total), f32),
                pltpu.VMEM((1, width), f32),
                pltpu.VMEM((4, *square), f32),
                pltpu.VMEM((powers, *square), bf16),
                pltpu.VMEM((powers, *square), bf16),
                pltpu.VMEM((powers, *square), bf16),
                pltpu.VMEM((powers, *square), bf16),
                pltpu.VMEM(square, bf16),
                pltpu.VMEM(square, bf16),
                pltpu.VMEM(square, bf16),
                pltpu.VMEM(square, bf16),
                pltpu.VMEM((nc, steps, width), f32),
                pltpu.VMEM((nc, steps, width), f32),
                pltpu.VMEM((nx, steps, width), f32),
                pltpu.VMEM((nz, 1, width), f32),
                pltpu.VMEM((nz, 1, width), f32),
                pltpu.VMEM((total, 1), f32),
                pltpu.VMEM((total, width), f32),
                pltpu.VMEM((total, width), f32),
                pltpu.VMEM((nx, steps, width), f32),
                pltpu.VMEM((nx, steps, width), f32),
                pltpu.VMEM((nx, steps, width), f32),
                pltpu.VMEM((blocks, steps, BLOCK), f32),
                pltpu.VMEM((blocks, steps, BLOCK), f32),
                pltpu.VMEM((nc, steps, BLOCK), f32),
                pltpu.VMEM((nc, steps, BLOCK), f32),
                dma((10,)),
                dma((nc,)), dma((nc,)),
                dma((nx,)), dma((nx,)),
                dma((nz,)), dma((nz,)),
                dma((nz,)), dma((nz,)),
                dma((nc,)), dma((nc,)),
                dma((nc,)), dma((nc,)),
            ],
            compiler_params=pltpu.CompilerParams(
                collective_id=0, has_side_effects=True, vmem_limit_bytes=LIMIT
            ),
        )(
            observations, obs_matrix, block_pattern, noise_precision.reshape(1, channels),
            retention, prior_mean.reshape(1, width),
            filter_matrix, filter_gain, transition, smoother_gain,
        )
        odd = lax.rem(lax.axis_index("chan"), 2) == 1
        half = BLOCK // 2
        return tuple(jnp.where(odd, array[:, :, half:], array[:, :, :half]) for array in both)

    placed = (
        P(None, "tm", "chan"), P("chan", None), P("chan", None), P("chan"),
        P(), P(), P(), P(), P(), P(),
    )
    return jax.shard_map(
        per_device,
        mesh=mesh,
        in_specs=placed,
        out_specs=(P(None, "tm", "chan"), P(None, "tm", "chan")),
        check_vma=False,
    )


def solution(mesh):
    return build(mesh, PLANE)
```

```python
import functools

import jax
import jax.numpy as jnp
from jax import lax
from jax.experimental import pallas as pl
from jax.experimental.pallas import tpu as pltpu
from jax.sharding import PartitionSpec as P

BLOCK = 128
PLANE = 4
NEAR = 2
LIMIT = 63 * 1024 * 1024
MESH = pl.DeviceIdType.MESH
f32 = jnp.float32
bf16 = jnp.bfloat16


def dot(a, b):
    return jnp.dot(a, b, preferred_element_type=f32)


def split(x):
    high = x.astype(bf16)
    return high, (x - high.astype(f32)).astype(bf16)


def times(x, high, low):
    rows = x.shape[0]
    if rows % 16:
        x_high = x.astype(bf16).astype(f32)
        both = jnp.concatenate([x_high, x - x_high], 0).astype(bf16)
        first, second = dot(both, high), dot(both, low)
        return first[:rows] + (first[rows:] + second[:rows])
    x_high, x_low = split(x)
    if rows >= 256:
        return dot(x_high, high) + (dot(x_low, high) + dot(x_high, low))
    first = dot(jnp.concatenate([x_high, x_low], 0), high)
    return first[:rows] + (first[rows:] + dot(x_high, low))


def shifted(x, distance):
    return jnp.roll(x, distance, axis=0)


def kernel(
    nx, nz, nc, steps, width, channels,
    obs_hbm, mat_hbm, pattern_hbm, noise_hbm, retention_hbm, prior_hbm, f_hbm, k_hbm, t_hbm, g_hbm,
    filtered, smoothed,
    obs, mat, pattern, noise, retention, prior, raw, fgh, fgl, wh, wl, kh, kl,
    own_power, other_power, part, part_in, drive, ends, starts, rho, rows_y, rows_c, fbuf, cbuf, bbuf,
    out_f, out_s, in_f, in_s,
    load_sem, rs_send, rs_recv, x_send, x_recv, e_send, e_recv, b_send, b_recv,
    of_send, of_recv, os_send, os_recv, pow_send, pow_recv, ready,
):
    tm, chan = lax.axis_index("tm"), lax.axis_index("chan")
    z, x = tm // nx, tm % nx
    span = nx * steps
    total = nz * span
    local_bits = span.bit_length() - 1
    z_bits = nz.bit_length() - 1

    loads = [
        pltpu.make_async_copy(source, target, load_sem.at[i])
        for i, (source, target) in enumerate(
            (
                (obs_hbm, obs),
                (mat_hbm, mat),
                (pattern_hbm, pattern),
                (noise_hbm, noise),
                (f_hbm, raw.at[0]),
                (k_hbm, raw.at[1]),
                (g_hbm, raw.at[2]),
                (t_hbm, raw.at[3]),
                (retention_hbm, retention),
                (prior_hbm, prior),
            )
        )
    ]
    for load in loads:
        load.start()

    def chan_peer(i):
        return {"chan": lax.rem(chan + i, nc)}

    def x_peer(i):
        return {"tm": z * nx + lax.rem(x + i, nx)}

    def z_peer(i):
        return {"tm": lax.rem(z + i, nz) * nx + x}

    near = [i for i in range(1, nz) if min(i, nz - i) <= NEAR]
    barrier = pltpu.get_barrier_semaphore()
    for i in near:
        pl.semaphore_signal(barrier, inc=1, device_id=z_peer(i), device_id_type=MESH)
    for i in range(1, nx):
        pl.semaphore_signal(barrier, inc=1, device_id=x_peer(i), device_id_type=MESH)
    for i in range(1, nc):
        pl.semaphore_signal(barrier, inc=1, device_id=chan_peer(i), device_id_type=MESH)

    def ring(distance):
        return sorted({i for i in (distance, nz - distance) if 0 < i < nz})

    rounds = [d for d in (NEAR, 2 * NEAR) if 2 * d <= nz // 2]

    def widen(k):
        for i in ring(rounds[k]):
            pl.semaphore_signal(ready.at[k], inc=1, device_id=z_peer(i), device_id_type=MESH)

    def widened(k):
        pl.semaphore_wait(ready.at[k], len(ring(rounds[k])))

    def remote(source, target, send, recv, peer):
        return pltpu.make_async_remote_copy(
            src_ref=source, dst_ref=target, send_sem=send, recv_sem=recv,
            device_id=peer, device_id_type=MESH,
        )

    fh, fl, gh, gl = fgh.at[0], fgl.at[0], fgh.at[1], fgl.at[1]
    core = lax.rem(chan, 2)
    twin = {"chan": chan + 1 - 2 * core}

    def power_copy(i):
        return remote(own_power.at[i], other_power.at[i], pow_send.at[i], pow_recv.at[i], twin)

    def square(first, last):
        def body(i, _):
            a, b = fgh[core, i], fgl[core, i]
            product = dot(a, a) + (dot(a, b) + dot(b, a))
            own_power[i] = product
            h, l = split(product)
            fgh[core, i + 1] = h
            fgl[core, i + 1] = l
            return 0

        lax.fori_loop(first, last, body, 0)

    def send_powers(first, last):
        for i in range(first, last):
            power_copy(i).start()

    def take_powers(first, last):
        def body(i, _):
            power_copy(i).wait_recv()
            h, l = split(other_power[i])
            fgh[1 - core, i + 1] = h
            fgl[1 - core, i + 1] = l
            return 0

        lax.fori_loop(first, last, body, 0)

    for load in loads[:4]:
        load.wait()
    weighted = obs[...].astype(f32) * noise[...].reshape(1, 1, channels)
    weighted = weighted.reshape(nc * steps, channels).astype(bf16)
    lane_block = lax.broadcasted_iota(jnp.int32, (BLOCK, width), 1) // BLOCK
    used = []
    for i in range(channels // BLOCK):
        mask = jnp.zeros((BLOCK, width), f32)
        for j in range(width // BLOCK):
            mask = jnp.where(lane_block == j, pattern[i, j].astype(f32), mask)
        used.append(mat[i * BLOCK : (i + 1) * BLOCK] * mask.astype(bf16))
    part[...] = dot(weighted, jnp.concatenate(used, 0)).reshape(nc, steps, width)

    loads[4].wait()
    loads[6].wait()
    for which in range(2):
        fgh[which, 0], fgl[which, 0] = split(raw[2 * which])
    square(0, 2)

    pl.semaphore_wait(barrier, len(near) + nx + nc - 2)
    sums = []
    for i in range(1, nc):
        there = lax.rem(chan + i, nc)
        copy = remote(part.at[there], part_in.at[chan], rs_send.at[i], rs_recv.at[i], chan_peer(i))
        copy.start()
        sums.append(copy)
    part_in[chan] = part[chan]
    send_powers(0, 2)
    if rounds:
        widen(0)

    loads[8].wait()
    loads[9].wait()
    row = retention[pl.ds(chan, 1), :]
    index = lax.broadcasted_iota(jnp.int32, (total, 1), 0)
    plane, rest = index % nz, index // nz
    wanted = plane * span + (rest % nx) * steps + rest // nx
    there = lax.broadcasted_iota(jnp.int32, (total, total), 1)
    column = jnp.sum(jnp.where(there == wanted, row, 0.0), axis=1, keepdims=True)

    def rows_of(t):
        start = ((t % steps) * nx + t // steps) * nz
        return slice(start, start + nz)

    running = column[:nz]
    rho[:nz] = running
    for t in range(1, span):
        running = running * column[rows_of(t)]
        rho[rows_of(t)] = running
    block_row = lax.broadcasted_iota(jnp.int32, (nz, 1), 0)
    chain = jnp.where(block_row >= 1, shifted(running, 1), 0.0)
    block_factors = [chain]
    for level in range(1, z_bits):
        chain = chain * shifted(chain, 1 << (level - 1))
        block_factors.append(jnp.where(block_row >= (1 << level), chain, 0.0))
    step_row = lax.broadcasted_iota(jnp.int32, (span, 1), 0)
    here = lax.broadcasted_iota(jnp.int32, (span, total), 0)
    there = lax.broadcasted_iota(jnp.int32, (span, total), 1)
    own = jnp.sum(jnp.where(there == here + z * span, row, 0.0), axis=1, keepdims=True)
    own_factors = [jnp.where(step_row >= 1, own, 0.0)]
    for level in range(1, local_bits):
        own = own * shifted(own, 1 << (level - 1))
        own_factors.append(jnp.where(step_row >= (1 << level), own, 0.0))

    loads[5].wait()
    kh[...], kl[...] = split(raw[1])
    square(2, 4)
    send_powers(2, 4)
    square(4, 5)
    send_powers(4, 5)

    loads[7].wait()
    th, tl = split(raw[3])
    eye = lax.broadcasted_iota(jnp.int32, (width, width), 0) == lax.broadcasted_iota(
        jnp.int32, (width, width), 1
    )
    product = dot(th, gh[0]) + (dot(th, gl[0]) + dot(tl, gh[0]))
    wh[...], wl[...] = split(jnp.where(eye, 1.0, 0.0) - product)

    for copy in sums:
        copy.wait()
    if rounds:
        widened(0)
    if len(rounds) > 1:
        widen(1)
    information = part_in[0]
    for i in range(1, nc):
        information = information + part_in[i]
    drive[x] = times(information, kh[...], kl[...])
    spread = []
    for i in range(1, nx):
        copy = remote(drive.at[x], drive.at[x], x_send.at[i], x_recv.at[i], x_peer(i))
        copy.start()
        spread.append(copy)

    square(5, local_bits + z_bits - 1)
    send_powers(5, local_bits + z_bits - 1)
    take_powers(0, 4)

    for copy in spread:
        copy.wait()
    if len(rounds) > 1:
        widened(1)

    local = drive[...].reshape(span, width)
    for level in range(local_bits):
        moved = shifted(local, 1 << level)
        local = local + own_factors[level] * times(moved, fh[level], fl[level])
    ends[z] = local[span - 1 :]
    fbuf[...] = local.reshape(nx, steps, width)
    across = []
    for i in sorted(range(1, nz), key=lambda i: -min(i, nz - i)):
        copy = remote(ends.at[z], ends.at[z], e_send.at[i], e_recv.at[i], z_peer(i))
        copy.start()
        across.append(copy)

    last_plane = z == nz - 1
    corrected = times(local, wh[...], wl[...])
    corrected = jnp.where(last_plane & (step_row == span - 1), local, corrected)
    cbuf[...] = corrected.reshape(nx, steps, width)
    backward = corrected
    for level in (2, 1, 0):
        backward = backward + times(shifted(backward, -(1 << level)), gh[level], gl[level])
    bbuf[...] = backward.reshape(nx, steps, width)
    for level in range(local_bits - 1, 2, -1):
        backward = backward + times(shifted(backward, -(1 << level)), gh[level], gl[level])
    starts[z] = backward[:1]
    for i in sorted(range(1, nz), key=lambda i: -min(i, nz - i)):
        copy = remote(starts.at[z], starts.at[z], b_send.at[i], b_recv.at[i], z_peer(i))
        copy.start()
        across.append(copy)

    take_powers(4, local_bits + z_bits - 1)

    for copy in across[: nz - 1]:
        copy.wait()

    carry = jnp.where(block_row == 0, prior[...], shifted(ends[...].reshape(nz, width), 1))
    for level in range(z_bits):
        moved = shifted(carry, 1 << level)
        high, low = fh[local_bits + level], fl[local_bits + level]
        carry = carry + block_factors[level] * times(moved, high, low)

    rows_y[:nz] = times(carry, fh[0], fl[0])
    count = nz
    for level in (*range(3, local_bits), 0, 1, 2):
        rows_y[count : 2 * count] = times(rows_y[:count], fh[level], fl[level])
        count = 2 * count
    rows_y[...] = rows_y[...] * rho[...]

    def own_rows(rows):
        return jnp.concatenate([rows[pl.ds((p * nx + x) * nz + z, 1), :] for p in range(steps)], 0)

    def send_out(state, out, into, send, recv):
        copies = []
        for k in range(width // BLOCK):
            out[k] = state[:, k * BLOCK : (k + 1) * BLOCK]
        for i in range(1, nc):
            there = lax.rem(chan + i, nc)
            copy = remote(out.at[there // 2], into.at[chan], send.at[i], recv.at[i], chan_peer(i))
            copy.start()
            copies.append(copy)
        into[chan] = out[chan // 2]
        return copies

    copies_f = send_out(fbuf[x] + own_rows(rows_y), out_f, in_f, of_send, of_recv)

    rows_c[...] = times(rows_y[...], wh[...], wl[...])
    rows_c[total - 1 :] = rows_y[total - 1 :]
    own_corrected = cbuf[x] + own_rows(rows_c)

    for level in (2, 1, 0):
        half = nx * nz << level
        rows_c[:half] = rows_c[:half] + times(rows_c[half : 2 * half], gh[level], gl[level])

    for copy in across[nz - 1 :]:
        copy.wait()
    whole = block_row == z
    for q in range(nx):
        own_start = bbuf[q][:1]
        if q == 0:
            extra = jnp.where(whole, own_start, starts[...].reshape(nz, width))
        else:
            extra = jnp.where(whole, own_start, 0.0)
        value = rows_c[q * nz : (q + 1) * nz] + extra
        rows_y[q * nz : (q + 1) * nz] = value
        later = jnp.where(block_row < nz - 1, shifted(value, -1), 0.0)
        rows_y[(nx + q) * nz : (nx + q + 1) * nz] = later
    first = pl.multiple_of((1 + x) * nz, nz)
    tail = rows_y[pl.ds(first, nx * nz), :]
    for level in range(local_bits - 1, 2, -1):
        half = nz << (level - 3)
        tail = tail[:half] + times(tail[half:], gh[level], gl[level])
    for level in range(z_bits):
        distance = 1 << level
        moved = jnp.where(block_row < nz - distance, shifted(tail, -distance), 0.0)
        high, low = gh[local_bits + level], gl[local_bits + level]
        tail = tail + times(moved, high, low)
    after = jnp.sum(jnp.where(whole, tail, 0.0), axis=0, keepdims=True)

    row8 = lax.broadcasted_iota(jnp.int32, (steps, 1), 0)
    placed = jnp.where(row8 == steps - 1, after, 0.0)
    state = own_corrected + times(placed, gh[0], gl[0])
    for level in range(3):
        distance = 1 << level
        moved = jnp.where(row8 < steps - distance, shifted(state, -distance), 0.0)
        state = state + times(moved, gh[level], gl[level])
    copies_s = send_out(state, out_s, in_s, os_send, os_recv)

    for i in range(local_bits + z_bits - 1):
        power_copy(i).wait_send()
    for copies, into, result in ((copies_f, in_f, filtered), (copies_s, in_s, smoothed)):
        for copy in copies:
            copy.wait()
        result[...] = into[...]


def build(mesh, nx):
    nc = mesh.shape["chan"]
    nz = mesh.shape["tm"] // nx

    def per_device(
        observations, obs_matrix, block_pattern, noise_precision, retention, prior_mean,
        filter_matrix, filter_gain, transition, smoother_gain,
    ):
        series, steps, channels = observations.shape
        width = obs_matrix.shape[1]
        span = nx * steps
        total = span * nz
        powers = total.bit_length() - 1
        vmem = pl.BlockSpec(memory_space=pltpu.VMEM)
        hbm = pl.BlockSpec(memory_space=pl.ANY)
        dma = pltpu.SemaphoreType.DMA
        square = (width, width)
        blocks = width // BLOCK
        result = jax.ShapeDtypeStruct((series, steps, BLOCK), f32)
        both = pl.pallas_call(
            functools.partial(kernel, nx, nz, nc, steps, width, channels),
            out_shape=(result, result),
            in_specs=[hbm] * 10,
            out_specs=(vmem, vmem),
            scratch_shapes=[
                pltpu.VMEM((series, steps, channels), bf16),
                pltpu.VMEM((channels, width), bf16),
                pltpu.SMEM((channels // BLOCK, width // BLOCK), jnp.int32),
                pltpu.VMEM((1, channels), f32),
                pltpu.VMEM((series, total), f32),
                pltpu.VMEM((1, width), f32),
                pltpu.VMEM((4, *square), f32),
                pltpu.VMEM((2, powers, *square), bf16),
                pltpu.VMEM((2, powers, *square), bf16),
                pltpu.VMEM(square, bf16),
                pltpu.VMEM(square, bf16),
                pltpu.VMEM(square, bf16),
                pltpu.VMEM(square, bf16),
                pltpu.VMEM((powers - 1, *square), f32),
                pltpu.VMEM((powers - 1, *square), f32),
                pltpu.VMEM((nc, steps, width), f32),
                pltpu.VMEM((nc, steps, width), f32),
                pltpu.VMEM((nx, steps, width), f32),
                pltpu.VMEM((nz, 1, width), f32),
                pltpu.VMEM((nz, 1, width), f32),
                pltpu.VMEM((total, 1), f32),
                pltpu.VMEM((total, width), f32),
                pltpu.VMEM((total, width), f32),
                pltpu.VMEM((nx, steps, width), f32),
                pltpu.VMEM((nx, steps, width), f32),
                pltpu.VMEM((nx, steps, width), f32),
                pltpu.VMEM((blocks, steps, BLOCK), f32),
                pltpu.VMEM((blocks, steps, BLOCK), f32),
                pltpu.VMEM((nc, steps, BLOCK), f32),
                pltpu.VMEM((nc, steps, BLOCK), f32),
                dma((10,)),
                dma((nc,)), dma((nc,)),
                dma((nx,)), dma((nx,)),
                dma((nz,)), dma((nz,)),
                dma((nz,)), dma((nz,)),
                dma((nc,)), dma((nc,)),
                dma((nc,)), dma((nc,)),
                dma((powers,)), dma((powers,)),
                pltpu.SemaphoreType.REGULAR((2,)),
            ],
            compiler_params=pltpu.CompilerParams(
                collective_id=0, has_side_effects=True, vmem_limit_bytes=LIMIT
            ),
        )(
            observations, obs_matrix, block_pattern, noise_precision.reshape(1, channels),
            retention, prior_mean.reshape(1, width),
            filter_matrix, filter_gain, transition, smoother_gain,
        )
        odd = lax.rem(lax.axis_index("chan"), 2) == 1
        half = BLOCK // 2
        return tuple(jnp.where(odd, array[:, :, half:], array[:, :, :half]) for array in both)

    placed = (
        P(None, "tm", "chan"), P("chan", None), P("chan", None), P("chan"),
        P(), P(), P(), P(), P(), P(),
    )
    return jax.shard_map(
        per_device,
        mesh=mesh,
        in_specs=placed,
        out_specs=(P(None, "tm", "chan"), P(None, "tm", "chan")),
        check_vma=False,
    )


def solution(mesh):
    return build(mesh, PLANE)
```

```python
import functools

import jax
import jax.numpy as jnp
from jax import lax
from jax.experimental import pallas as pl
from jax.experimental.pallas import tpu as pltpu
from jax.sharding import PartitionSpec as P

BLOCK = 128
PLANE = 4
NEAR = 2
LIMIT = 63 * 1024 * 1024
MESH = pl.DeviceIdType.MESH
f32 = jnp.float32
bf16 = jnp.bfloat16


def dot(a, b):
    return jnp.dot(a, b, preferred_element_type=f32)


def split(x):
    high = x.astype(bf16)
    return high, (x - high.astype(f32)).astype(bf16)


def times(x, high, low):
    rows = x.shape[0]
    if rows % 16:
        x_high = x.astype(bf16).astype(f32)
        both = jnp.concatenate([x_high, x - x_high], 0).astype(bf16)
        first, second = dot(both, high), dot(both, low)
        return first[:rows] + (first[rows:] + second[:rows])
    x_high, x_low = split(x)
    if rows >= 256:
        return dot(x_high, high) + (dot(x_low, high) + dot(x_high, low))
    first = dot(jnp.concatenate([x_high, x_low], 0), high)
    return first[:rows] + (first[rows:] + dot(x_high, low))


def shifted(x, distance):
    return jnp.roll(x, distance, axis=0)


def kernel(
    nx, nz, nc, steps, width, channels,
    obs_hbm, mat_hbm, pattern_hbm, noise_hbm, retention_hbm, prior_hbm, f_hbm, k_hbm, t_hbm, g_hbm,
    filtered, smoothed,
    obs, mat, pattern, noise, retention, prior, raw, fgh, fgl, wh, wl, kh, kl,
    own_power, other_power, part, part_in, drive, ends, starts, rho, rows_y, rows_c, fbuf, cbuf, bbuf,
    out_f, out_s, in_f, in_s,
    load_sem, rs_send, rs_recv, x_send, x_recv, e_send, e_recv, b_send, b_recv,
    of_send, of_recv, os_send, os_recv, pow_send, pow_recv, ready,
):
    tm, chan = lax.axis_index("tm"), lax.axis_index("chan")
    z, x = tm // nx, tm % nx
    span = nx * steps
    total = nz * span
    local_bits = span.bit_length() - 1
    z_bits = nz.bit_length() - 1

    loads = [
        pltpu.make_async_copy(source, target, load_sem.at[i])
        for i, (source, target) in enumerate(
            (
                (obs_hbm, obs),
                (mat_hbm, mat),
                (pattern_hbm, pattern),
                (noise_hbm, noise),
                (f_hbm, raw.at[0]),
                (k_hbm, raw.at[1]),
                (g_hbm, raw.at[2]),
                (t_hbm, raw.at[3]),
                (retention_hbm, retention),
                (prior_hbm, prior),
            )
        )
    ]
    for load in loads:
        load.start()

    def chan_peer(i):
        return {"chan": lax.rem(chan + i, nc)}

    def x_peer(i):
        return {"tm": z * nx + lax.rem(x + i, nx)}

    def z_peer(i):
        return {"tm": lax.rem(z + i, nz) * nx + x}

    near = [i for i in range(1, nz) if min(i, nz - i) <= NEAR]
    barrier = pltpu.get_barrier_semaphore()
    for i in near:
        pl.semaphore_signal(barrier, inc=1, device_id=z_peer(i), device_id_type=MESH)
    for i in range(1, nx):
        pl.semaphore_signal(barrier, inc=1, device_id=x_peer(i), device_id_type=MESH)
    for i in range(1, nc):
        pl.semaphore_signal(barrier, inc=1, device_id=chan_peer(i), device_id_type=MESH)

    def ring(distance):
        return sorted({i for i in (distance, nz - distance) if 0 < i < nz})

    rounds = [d for d in (NEAR, 2 * NEAR) if 2 * d <= nz // 2]

    def widen(k):
        for i in ring(rounds[k]):
            pl.semaphore_signal(ready.at[k], inc=1, device_id=z_peer(i), device_id_type=MESH)

    def widened(k):
        pl.semaphore_wait(ready.at[k], len(ring(rounds[k])))

    def remote(source, target, send, recv, peer):
        return pltpu.make_async_remote_copy(
            src_ref=source, dst_ref=target, send_sem=send, recv_sem=recv,
            device_id=peer, device_id_type=MESH,
        )

    fh, fl, gh, gl = fgh.at[0], fgl.at[0], fgh.at[1], fgl.at[1]
    core = lax.rem(chan, 2)
    twin = {"chan": chan + 1 - 2 * core}

    def power_copy(i):
        return remote(own_power.at[i], other_power.at[i], pow_send.at[i], pow_recv.at[i], twin)

    def square(first, last, send=True):
        def body(i, _):
            a, b = fgh[core, i], fgl[core, i]
            product = dot(a, a) + (dot(a, b) + dot(b, a))
            own_power[i] = product
            if send:
                power_copy(i).start()
            h, l = split(product)
            fgh[core, i + 1] = h
            fgl[core, i + 1] = l
            return 0

        lax.fori_loop(first, last, body, 0)

    def send_powers(first, last):
        for i in range(first, last):
            power_copy(i).start()

    def take_powers(first, last):
        def body(i, _):
            power_copy(i).wait_recv()
            h, l = split(other_power[i])
            fgh[1 - core, i + 1] = h
            fgl[1 - core, i + 1] = l
            return 0

        lax.fori_loop(first, last, body, 0)

    for load in loads[:4]:
        load.wait()
    weighted = obs[...].astype(f32) * noise[...].reshape(1, 1, channels)
    weighted = weighted.reshape(nc * steps, channels).astype(bf16)
    lane_block = lax.broadcasted_iota(jnp.int32, (BLOCK, width), 1) // BLOCK
    used = []
    for i in range(channels // BLOCK):
        mask = jnp.zeros((BLOCK, width), f32)
        for j in range(width // BLOCK):
            mask = jnp.where(lane_block == j, pattern[i, j].astype(f32), mask)
        used.append(mat[i * BLOCK : (i + 1) * BLOCK] * mask.astype(bf16))
    part[...] = dot(weighted, jnp.concatenate(used, 0)).reshape(nc, steps, width)

    loads[4].wait()
    loads[6].wait()
    fgh[core, 0], fgl[core, 0] = split(raw[2 * core])
    square(0, 1, send=False)

    pl.semaphore_wait(barrier, len(near) + nx + nc - 2)
    sums = []
    for i in range(1, nc):
        there = lax.rem(chan + i, nc)
        copy = remote(part.at[there], part_in.at[chan], rs_send.at[i], rs_recv.at[i], chan_peer(i))
        copy.start()
        sums.append(copy)
    part_in[chan] = part[chan]
    send_powers(0, 1)
    if rounds:
        widen(0)
    square(1, 4)
    fgh[1 - core, 0], fgl[1 - core, 0] = split(raw[2 * (1 - core)])

    loads[8].wait()
    loads[9].wait()
    row = retention[pl.ds(chan, 1), :]
    index = lax.broadcasted_iota(jnp.int32, (total, 1), 0)
    plane, rest = index % nz, index // nz
    wanted = plane * span + (rest % nx) * steps + rest // nx
    there = lax.broadcasted_iota(jnp.int32, (total, total), 1)
    column = jnp.sum(jnp.where(there == wanted, row, 0.0), axis=1, keepdims=True)

    def rows_of(t):
        start = ((t % steps) * nx + t // steps) * nz
        return slice(start, start + nz)

    running = column[:nz]
    rho[:nz] = running
    for t in range(1, span):
        running = running * column[rows_of(t)]
        rho[rows_of(t)] = running
    block_row = lax.broadcasted_iota(jnp.int32, (nz, 1), 0)
    chain = jnp.where(block_row >= 1, shifted(running, 1), 0.0)
    block_factors = [chain]
    for level in range(1, z_bits):
        chain = chain * shifted(chain, 1 << (level - 1))
        block_factors.append(jnp.where(block_row >= (1 << level), chain, 0.0))
    step_row = lax.broadcasted_iota(jnp.int32, (span, 1), 0)
    here = lax.broadcasted_iota(jnp.int32, (span, total), 0)
    there = lax.broadcasted_iota(jnp.int32, (span, total), 1)
    own = jnp.sum(jnp.where(there == here + z * span, row, 0.0), axis=1, keepdims=True)
    own_factors = [jnp.where(step_row >= 1, own, 0.0)]
    for level in range(1, local_bits):
        own = own * shifted(own, 1 << (level - 1))
        own_factors.append(jnp.where(step_row >= (1 << level), own, 0.0))

    loads[5].wait()
    kh[...], kl[...] = split(raw[1])


    for copy in sums:
        copy.wait()
    information = part_in[0]
    for i in range(1, nc):
        information = information + part_in[i]
    drive[x] = times(information, kh[...], kl[...])
    spread = []
    for i in range(1, nx):
        copy = remote(drive.at[x], drive.at[x], x_send.at[i], x_recv.at[i], x_peer(i))
        copy.start()
        spread.append(copy)

    if rounds:
        widened(0)
    if len(rounds) > 1:
        widen(1)
    loads[7].wait()
    th, tl = split(raw[3])
    eye = lax.broadcasted_iota(jnp.int32, (width, width), 0) == lax.broadcasted_iota(
        jnp.int32, (width, width), 1
    )
    product = dot(th, gh[0]) + (dot(th, gl[0]) + dot(tl, gh[0]))
    wh[...], wl[...] = split(jnp.where(eye, 1.0, 0.0) - product)
    take_powers(0, 4)
    square(4, 5)

    for copy in spread:
        copy.wait()
    if len(rounds) > 1:
        widened(1)

    local = drive[...].reshape(span, width)
    for level in range(local_bits):
        moved = shifted(local, 1 << level)
        local = local + own_factors[level] * times(moved, fh[level], fl[level])
    ends[z] = local[span - 1 :]
    fbuf[...] = local.reshape(nx, steps, width)
    across = []
    for i in sorted(range(1, nz), key=lambda i: -min(i, nz - i)):
        copy = remote(ends.at[z], ends.at[z], e_send.at[i], e_recv.at[i], z_peer(i))
        copy.start()
        across.append(copy)

    square(5, local_bits + z_bits - 1)

    last_plane = z == nz - 1
    corrected = times(local, wh[...], wl[...])
    corrected = jnp.where(last_plane & (step_row == span - 1), local, corrected)
    cbuf[...] = corrected.reshape(nx, steps, width)
    backward = corrected
    for level in (2, 1, 0):
        backward = backward + times(shifted(backward, -(1 << level)), gh[level], gl[level])
    bbuf[...] = backward.reshape(nx, steps, width)
    for level in range(local_bits - 1, 2, -1):
        backward = backward + times(shifted(backward, -(1 << level)), gh[level], gl[level])
    starts[z] = backward[:1]
    for i in sorted(range(1, nz), key=lambda i: -min(i, nz - i)):
        copy = remote(starts.at[z], starts.at[z], b_send.at[i], b_recv.at[i], z_peer(i))
        copy.start()
        across.append(copy)

    take_powers(4, local_bits + z_bits - 1)

    for copy in across[: nz - 1]:
        copy.wait()

    carry = jnp.where(block_row == 0, prior[...], shifted(ends[...].reshape(nz, width), 1))
    for level in range(z_bits):
        moved = shifted(carry, 1 << level)
        high, low = fh[local_bits + level], fl[local_bits + level]
        carry = carry + block_factors[level] * times(moved, high, low)

    rows_y[:nz] = times(carry, fh[0], fl[0])
    count = nz
    for level in (*range(3, local_bits), 0, 1, 2):
        rows_y[count : 2 * count] = times(rows_y[:count], fh[level], fl[level])
        count = 2 * count
    rows_y[...] = rows_y[...] * rho[...]

    def own_rows(rows):
        return jnp.concatenate([rows[pl.ds((p * nx + x) * nz + z, 1), :] for p in range(steps)], 0)

    def send_out(state, out, into, send, recv):
        copies = []
        for k in range(width // BLOCK):
            out[k] = state[:, k * BLOCK : (k + 1) * BLOCK]
        for i in range(1, nc):
            there = lax.rem(chan + i, nc)
            copy = remote(out.at[there // 2], into.at[chan], send.at[i], recv.at[i], chan_peer(i))
            copy.start()
            copies.append(copy)
        into[chan] = out[chan // 2]
        return copies

    copies_f = send_out(fbuf[x] + own_rows(rows_y), out_f, in_f, of_send, of_recv)

    rows_c[...] = times(rows_y[...], wh[...], wl[...])
    rows_c[total - 1 :] = rows_y[total - 1 :]
    own_corrected = cbuf[x] + own_rows(rows_c)

    for level in (2, 1, 0):
        half = nx * nz << level
        rows_c[:half] = rows_c[:half] + times(rows_c[half : 2 * half], gh[level], gl[level])

    for copy in across[nz - 1 :]:
        copy.wait()
    whole = block_row == z
    for q in range(nx):
        own_start = bbuf[q][:1]
        if q == 0:
            extra = jnp.where(whole, own_start, starts[...].reshape(nz, width))
        else:
            extra = jnp.where(whole, own_start, 0.0)
        value = rows_c[q * nz : (q + 1) * nz] + extra
        rows_y[q * nz : (q + 1) * nz] = value
        later = jnp.where(block_row < nz - 1, shifted(value, -1), 0.0)
        rows_y[(nx + q) * nz : (nx + q + 1) * nz] = later
    first = pl.multiple_of((1 + x) * nz, nz)
    tail = rows_y[pl.ds(first, nx * nz), :]
    for level in range(local_bits - 1, 2, -1):
        half = nz << (level - 3)
        tail = tail[:half] + times(tail[half:], gh[level], gl[level])
    for level in range(z_bits):
        distance = 1 << level
        moved = jnp.where(block_row < nz - distance, shifted(tail, -distance), 0.0)
        high, low = gh[local_bits + level], gl[local_bits + level]
        tail = tail + times(moved, high, low)
    after = jnp.sum(jnp.where(whole, tail, 0.0), axis=0, keepdims=True)

    row8 = lax.broadcasted_iota(jnp.int32, (steps, 1), 0)
    placed = jnp.where(row8 == steps - 1, after, 0.0)
    state = own_corrected + times(placed, gh[0], gl[0])
    for level in range(3):
        distance = 1 << level
        moved = jnp.where(row8 < steps - distance, shifted(state, -distance), 0.0)
        state = state + times(moved, gh[level], gl[level])
    copies_s = send_out(state, out_s, in_s, os_send, os_recv)

    for i in range(local_bits + z_bits - 1):
        power_copy(i).wait_send()
    for copies, into, result in ((copies_f, in_f, filtered), (copies_s, in_s, smoothed)):
        for copy in copies:
            copy.wait()
        result[...] = into[...]


def build(mesh, nx):
    nc = mesh.shape["chan"]
    nz = mesh.shape["tm"] // nx

    def per_device(
        observations, obs_matrix, block_pattern, noise_precision, retention, prior_mean,
        filter_matrix, filter_gain, transition, smoother_gain,
    ):
        series, steps, channels = observations.shape
        width = obs_matrix.shape[1]
        span = nx * steps
        total = span * nz
        powers = total.bit_length() - 1
        vmem = pl.BlockSpec(memory_space=pltpu.VMEM)
        hbm = pl.BlockSpec(memory_space=pl.ANY)
        dma = pltpu.SemaphoreType.DMA
        square = (width, width)
        blocks = width // BLOCK
        result = jax.ShapeDtypeStruct((series, steps, BLOCK), f32)
        both = pl.pallas_call(
            functools.partial(kernel, nx, nz, nc, steps, width, channels),
            out_shape=(result, result),
            in_specs=[hbm] * 10,
            out_specs=(vmem, vmem),
            scratch_shapes=[
                pltpu.VMEM((series, steps, channels), bf16),
                pltpu.VMEM((channels, width), bf16),
                pltpu.SMEM((channels // BLOCK, width // BLOCK), jnp.int32),
                pltpu.VMEM((1, channels), f32),
                pltpu.VMEM((series, total), f32),
                pltpu.VMEM((1, width), f32),
                pltpu.VMEM((4, *square), f32),
                pltpu.VMEM((2, powers, *square), bf16),
                pltpu.VMEM((2, powers, *square), bf16),
                pltpu.VMEM(square, bf16),
                pltpu.VMEM(square, bf16),
                pltpu.VMEM(square, bf16),
                pltpu.VMEM(square, bf16),
                pltpu.VMEM((powers - 1, *square), f32),
                pltpu.VMEM((powers - 1, *square), f32),
                pltpu.VMEM((nc, steps, width), f32),
                pltpu.VMEM((nc, steps, width), f32),
                pltpu.VMEM((nx, steps, width), f32),
                pltpu.VMEM((nz, 1, width), f32),
                pltpu.VMEM((nz, 1, width), f32),
                pltpu.VMEM((total, 1), f32),
                pltpu.VMEM((total, width), f32),
                pltpu.VMEM((total, width), f32),
                pltpu.VMEM((nx, steps, width), f32),
                pltpu.VMEM((nx, steps, width), f32),
                pltpu.VMEM((nx, steps, width), f32),
                pltpu.VMEM((blocks, steps, BLOCK), f32),
                pltpu.VMEM((blocks, steps, BLOCK), f32),
                pltpu.VMEM((nc, steps, BLOCK), f32),
                pltpu.VMEM((nc, steps, BLOCK), f32),
                dma((10,)),
                dma((nc,)), dma((nc,)),
                dma((nx,)), dma((nx,)),
                dma((nz,)), dma((nz,)),
                dma((nz,)), dma((nz,)),
                dma((nc,)), dma((nc,)),
                dma((nc,)), dma((nc,)),
                dma((powers,)), dma((powers,)),
                pltpu.SemaphoreType.REGULAR((2,)),
            ],
            compiler_params=pltpu.CompilerParams(
                collective_id=0, has_side_effects=True, vmem_limit_bytes=LIMIT
            ),
        )(
            observations, obs_matrix, block_pattern, noise_precision.reshape(1, channels),
            retention, prior_mean.reshape(1, width),
            filter_matrix, filter_gain, transition, smoother_gain,
        )
        odd = lax.rem(lax.axis_index("chan"), 2) == 1
        half = BLOCK // 2
        return tuple(jnp.where(odd, array[:, :, half:], array[:, :, :half]) for array in both)

    placed = (
        P(None, "tm", "chan"), P("chan", None), P("chan", None), P("chan"),
        P(), P(), P(), P(), P(), P(),
    )
    return jax.shard_map(
        per_device,
        mesh=mesh,
        in_specs=placed,
        out_specs=(P(None, "tm", "chan"), P(None, "tm", "chan")),
        check_vma=False,
    )


def solution(mesh):
    return build(mesh, PLANE)
```

```python
import functools

import jax
import jax.numpy as jnp
from jax import lax
from jax.experimental import pallas as pl
from jax.experimental.pallas import tpu as pltpu
from jax.sharding import PartitionSpec as P

BLOCK = 128
PLANE = 4
NEAR = 2
LIMIT = 63 * 1024 * 1024
MESH = pl.DeviceIdType.MESH
f32 = jnp.float32
bf16 = jnp.bfloat16


def dot(a, b):
    return jnp.dot(a, b, preferred_element_type=f32)


def split(x):
    high = x.astype(bf16)
    return high, (x - high.astype(f32)).astype(bf16)


def times(x, high, low):
    rows = x.shape[0]
    if rows % 16:
        x_high = x.astype(bf16).astype(f32)
        both = jnp.concatenate([x_high, x - x_high], 0).astype(bf16)
        first, second = dot(both, high), dot(both, low)
        return first[:rows] + (first[rows:] + second[:rows])
    x_high, x_low = split(x)
    if rows >= 256:
        return dot(x_high, high) + (dot(x_low, high) + dot(x_high, low))
    first = dot(jnp.concatenate([x_high, x_low], 0), high)
    return first[:rows] + (first[rows:] + dot(x_high, low))


def shifted(x, distance):
    return jnp.roll(x, distance, axis=0)


def kernel(
    nx, nz, nc, steps, width, channels,
    obs_hbm, mat_hbm, pattern_hbm, noise_hbm, retention_hbm, prior_hbm, f_hbm, k_hbm, t_hbm, g_hbm,
    filtered, smoothed,
    obs, mat, pattern, noise, retention, prior, raw, fgh, fgl, wh, wl,
    own_power, other_power, part, part_in, drive, ends, starts, rho, rows_y, rows_c, fbuf, cbuf, bbuf,
    out_f, out_s, in_f, in_s,
    load_sem, rs_send, rs_recv, x_send, x_recv, e_send, e_recv, b_send, b_recv,
    of_send, of_recv, os_send, os_recv, pow_send, pow_recv, ready,
):
    tm, chan = lax.axis_index("tm"), lax.axis_index("chan")
    z, x = tm // nx, tm % nx
    span = nx * steps
    total = nz * span
    local_bits = span.bit_length() - 1
    z_bits = nz.bit_length() - 1

    loads = [
        pltpu.make_async_copy(source, target, load_sem.at[i])
        for i, (source, target) in enumerate(
            (
                (obs_hbm, obs),
                (mat_hbm, mat),
                (pattern_hbm, pattern),
                (noise_hbm, noise),
                (k_hbm, raw.at[1]),
                (f_hbm, raw.at[0]),
                (g_hbm, raw.at[2]),
                (t_hbm, raw.at[3]),
                (retention_hbm, retention),
                (prior_hbm, prior),
            )
        )
    ]
    for load in loads:
        load.start()

    def chan_peer(i):
        return {"chan": lax.rem(chan + i, nc)}

    def x_peer(i):
        return {"tm": z * nx + lax.rem(x + i, nx)}

    def z_peer(i):
        return {"tm": lax.rem(z + i, nz) * nx + x}

    near = [i for i in range(1, nz) if min(i, nz - i) <= NEAR]
    barrier = pltpu.get_barrier_semaphore()
    for i in range(1, nc):
        pl.semaphore_signal(barrier, inc=1, device_id=chan_peer(i), device_id_type=MESH)

    for i in range(1, nx):
        pl.semaphore_signal(barrier, inc=1, device_id=x_peer(i), device_id_type=MESH)
    for i in near:
        pl.semaphore_signal(barrier, inc=1, device_id=z_peer(i), device_id_type=MESH)

    def ring(distance):
        return sorted({i for i in (distance, nz - distance) if 0 < i < nz})

    rounds = [d for d in (NEAR, 2 * NEAR) if 2 * d <= nz // 2]

    def widen(k):
        for i in ring(rounds[k]):
            pl.semaphore_signal(ready.at[k], inc=1, device_id=z_peer(i), device_id_type=MESH)

    def widened(k):
        pl.semaphore_wait(ready.at[k], len(ring(rounds[k])))

    def far_first(count):
        return sorted(range(1, count), key=lambda i: -min(i, count - i))

    def remote(source, target, send, recv, peer):
        return pltpu.make_async_remote_copy(
            src_ref=source, dst_ref=target, send_sem=send, recv_sem=recv,
            device_id=peer, device_id_type=MESH,
        )

    fh, fl, gh, gl = fgh.at[0], fgl.at[0], fgh.at[1], fgl.at[1]
    core = lax.rem(chan, 2)
    twin = {"chan": chan + 1 - 2 * core}

    def power_copy(i):
        return remote(own_power.at[i], other_power.at[i], pow_send.at[i], pow_recv.at[i], twin)

    def square(first, last):
        def body(i, _):
            a, b = fgh[core, i], fgl[core, i]
            product = dot(a, a) + (dot(a, b) + dot(b, a))
            own_power[i] = product
            power_copy(i).start()
            h, l = split(product)
            fgh[core, i + 1] = h
            fgl[core, i + 1] = l
            return 0

        lax.fori_loop(first, last, body, 0)

    def take_powers(first, last):
        def body(i, _):
            power_copy(i).wait_recv()
            h, l = split(other_power[i])
            fgh[1 - core, i + 1] = h
            fgl[1 - core, i + 1] = l
            return 0

        lax.fori_loop(first, last, body, 0)

    for load in loads[:4]:
        load.wait()
    weighted = obs[...].astype(f32) * noise[...].reshape(1, 1, channels)
    weighted = weighted.reshape(nc * steps, channels).astype(bf16)
    lane_block = lax.broadcasted_iota(jnp.int32, (BLOCK, width), 1) // BLOCK
    used = []
    for i in range(channels // BLOCK):
        mask = jnp.zeros((BLOCK, width), f32)
        for j in range(width // BLOCK):
            mask = jnp.where(lane_block == j, pattern[i, j].astype(f32), mask)
        used.append(mat[i * BLOCK : (i + 1) * BLOCK] * mask.astype(bf16))
    information = dot(weighted, jnp.concatenate(used, 0))

    loads[4].wait()
    kh, kl = split(raw[1])
    part[...] = times(information, kh, kl).reshape(nc, steps, width)


    pl.semaphore_wait(barrier, len(near) + nx + nc - 2)
    sums = []
    for i in far_first(nc):
        there = lax.rem(chan + i, nc)
        copy = remote(part.at[there], part_in.at[chan], rs_send.at[i], rs_recv.at[i], chan_peer(i))
        copy.start()
        sums.append(copy)
    part_in[chan] = part[chan]
    if rounds:
        widen(0)
    loads[5].wait()
    loads[6].wait()
    fgh[core, 0], fgl[core, 0] = split(raw[2 * core])
    square(0, 3)

    loads[8].wait()
    loads[9].wait()
    row = retention[pl.ds(chan, 1), :]
    index = lax.broadcasted_iota(jnp.int32, (total, 1), 0)
    plane, rest = index % nz, index // nz
    wanted = plane * span + (rest % nx) * steps + rest // nx
    there = lax.broadcasted_iota(jnp.int32, (total, total), 1)
    column = jnp.sum(jnp.where(there == wanted, row, 0.0), axis=1, keepdims=True)

    def rows_of(t):
        start = ((t % steps) * nx + t // steps) * nz
        return slice(start, start + nz)

    running = column[:nz]
    rho[:nz] = running
    for t in range(1, span):
        running = running * column[rows_of(t)]
        rho[rows_of(t)] = running
    block_row = lax.broadcasted_iota(jnp.int32, (nz, 1), 0)
    chain = jnp.where(block_row >= 1, shifted(running, 1), 0.0)
    block_factors = [chain]
    for level in range(1, z_bits):
        chain = chain * shifted(chain, 1 << (level - 1))
        block_factors.append(jnp.where(block_row >= (1 << level), chain, 0.0))
    step_row = lax.broadcasted_iota(jnp.int32, (span, 1), 0)
    here = lax.broadcasted_iota(jnp.int32, (span, total), 0)
    there = lax.broadcasted_iota(jnp.int32, (span, total), 1)
    own = jnp.sum(jnp.where(there == here + z * span, row, 0.0), axis=1, keepdims=True)
    own_factors = [jnp.where(step_row >= 1, own, 0.0)]
    for level in range(1, local_bits):
        own = own * shifted(own, 1 << (level - 1))
        own_factors.append(jnp.where(step_row >= (1 << level), own, 0.0))


    for copy in sums:
        copy.wait()
    driving = part_in[0]
    for i in range(1, nc):
        driving = driving + part_in[i]
    drive[x] = driving
    spread = []
    for i in far_first(nx):
        copy = remote(drive.at[x], drive.at[x], x_send.at[i], x_recv.at[i], x_peer(i))
        copy.start()
        spread.append(copy)

    if rounds:
        widened(0)
    if len(rounds) > 1:
        widen(1)
    square(3, 4)
    fgh[1 - core, 0], fgl[1 - core, 0] = split(raw[2 * (1 - core)])
    loads[7].wait()
    th, tl = split(raw[3])
    eye = lax.broadcasted_iota(jnp.int32, (width, width), 0) == lax.broadcasted_iota(
        jnp.int32, (width, width), 1
    )
    product = dot(th, gh[0]) + (dot(th, gl[0]) + dot(tl, gh[0]))
    wh[...], wl[...] = split(jnp.where(eye, 1.0, 0.0) - product)
    take_powers(0, 4)

    for copy in spread:
        copy.wait()
    if len(rounds) > 1:
        widened(1)

    local = drive[...].reshape(span, width)
    for level in range(local_bits):
        moved = shifted(local, 1 << level)
        local = local + own_factors[level] * times(moved, fh[level], fl[level])
    ends[z] = local[span - 1 :]
    fbuf[...] = local.reshape(nx, steps, width)
    across = []
    for i in far_first(nz):
        copy = remote(ends.at[z], ends.at[z], e_send.at[i], e_recv.at[i], z_peer(i))
        copy.start()
        across.append(copy)

    square(4, local_bits + z_bits - 2)

    last_plane = z == nz - 1
    corrected = times(local, wh[...], wl[...])
    corrected = jnp.where(last_plane & (step_row == span - 1), local, corrected)
    cbuf[...] = corrected.reshape(nx, steps, width)
    backward = corrected
    for level in (2, 1, 0):
        backward = backward + times(shifted(backward, -(1 << level)), gh[level], gl[level])
    bbuf[...] = backward.reshape(nx, steps, width)
    for level in range(local_bits - 1, 2, -1):
        backward = backward + times(shifted(backward, -(1 << level)), gh[level], gl[level])
    starts[z] = backward[:1]
    for i in far_first(nz):
        copy = remote(starts.at[z], starts.at[z], b_send.at[i], b_recv.at[i], z_peer(i))
        copy.start()
        across.append(copy)

    square(local_bits + z_bits - 2, local_bits + z_bits - 1)
    take_powers(4, local_bits + z_bits - 1)

    for copy in across[: nz - 1]:
        copy.wait()

    carry = jnp.where(block_row == 0, prior[...], shifted(ends[...].reshape(nz, width), 1))
    for level in range(z_bits):
        moved = shifted(carry, 1 << level)
        high, low = fh[local_bits + level], fl[local_bits + level]
        carry = carry + block_factors[level] * times(moved, high, low)

    rows_y[:nz] = times(carry, fh[0], fl[0])
    count = nz
    for level in (*range(3, local_bits), 0, 1, 2):
        rows_y[count : 2 * count] = times(rows_y[:count], fh[level], fl[level])
        count = 2 * count
    rows_y[...] = rows_y[...] * rho[...]

    def own_rows(rows):
        return jnp.concatenate([rows[pl.ds((p * nx + x) * nz + z, 1), :] for p in range(steps)], 0)

    def send_out(state, out, into, send, recv):
        copies = []
        for k in range(width // BLOCK):
            out[k] = state[:, k * BLOCK : (k + 1) * BLOCK]
        for i in far_first(nc):
            there = lax.rem(chan + i, nc)
            copy = remote(out.at[there // 2], into.at[chan], send.at[i], recv.at[i], chan_peer(i))
            copy.start()
            copies.append(copy)
        into[chan] = out[chan // 2]
        return copies

    copies_f = send_out(fbuf[x] + own_rows(rows_y), out_f, in_f, of_send, of_recv)

    rows_c[...] = times(rows_y[...], wh[...], wl[...])
    rows_c[total - 1 :] = rows_y[total - 1 :]
    own_corrected = cbuf[x] + own_rows(rows_c)

    for level in (2, 1, 0):
        half = nx * nz << level
        rows_c[:half] = rows_c[:half] + times(rows_c[half : 2 * half], gh[level], gl[level])

    for copy in across[nz - 1 :]:
        copy.wait()
    whole = block_row == z
    for q in range(nx):
        own_start = bbuf[q][:1]
        if q == 0:
            extra = jnp.where(whole, own_start, starts[...].reshape(nz, width))
        else:
            extra = jnp.where(whole, own_start, 0.0)
        value = rows_c[q * nz : (q + 1) * nz] + extra
        rows_y[q * nz : (q + 1) * nz] = value
        later = jnp.where(block_row < nz - 1, shifted(value, -1), 0.0)
        rows_y[(nx + q) * nz : (nx + q + 1) * nz] = later
    first = pl.multiple_of((1 + x) * nz, nz)
    tail = rows_y[pl.ds(first, nx * nz), :]
    for level in range(local_bits - 1, 2, -1):
        half = nz << (level - 3)
        tail = tail[:half] + times(tail[half:], gh[level], gl[level])
    for level in range(z_bits):
        distance = 1 << level
        moved = jnp.where(block_row < nz - distance, shifted(tail, -distance), 0.0)
        high, low = gh[local_bits + level], gl[local_bits + level]
        tail = tail + times(moved, high, low)
    after = jnp.sum(jnp.where(whole, tail, 0.0), axis=0, keepdims=True)

    row8 = lax.broadcasted_iota(jnp.int32, (steps, 1), 0)
    placed = jnp.where(row8 == steps - 1, after, 0.0)
    state = own_corrected + times(placed, gh[0], gl[0])
    for level in range(3):
        distance = 1 << level
        moved = jnp.where(row8 < steps - distance, shifted(state, -distance), 0.0)
        state = state + times(moved, gh[level], gl[level])
    copies_s = send_out(state, out_s, in_s, os_send, os_recv)

    for i in range(local_bits + z_bits - 1):
        power_copy(i).wait_send()
    for copies, into, result in ((copies_f, in_f, filtered), (copies_s, in_s, smoothed)):
        for copy in copies:
            copy.wait()
        result[...] = into[...]


def build(mesh, nx):
    nc = mesh.shape["chan"]
    nz = mesh.shape["tm"] // nx

    def per_device(
        observations, obs_matrix, block_pattern, noise_precision, retention, prior_mean,
        filter_matrix, filter_gain, transition, smoother_gain,
    ):
        series, steps, channels = observations.shape
        width = obs_matrix.shape[1]
        span = nx * steps
        total = span * nz
        powers = total.bit_length() - 1
        vmem = pl.BlockSpec(memory_space=pltpu.VMEM)
        hbm = pl.BlockSpec(memory_space=pl.ANY)
        dma = pltpu.SemaphoreType.DMA
        square = (width, width)
        blocks = width // BLOCK
        result = jax.ShapeDtypeStruct((series, steps, BLOCK), f32)
        both = pl.pallas_call(
            functools.partial(kernel, nx, nz, nc, steps, width, channels),
            out_shape=(result, result),
            in_specs=[hbm] * 10,
            out_specs=(vmem, vmem),
            scratch_shapes=[
                pltpu.VMEM((series, steps, channels), bf16),
                pltpu.VMEM((channels, width), bf16),
                pltpu.SMEM((channels // BLOCK, width // BLOCK), jnp.int32),
                pltpu.VMEM((1, channels), f32),
                pltpu.VMEM((series, total), f32),
                pltpu.VMEM((1, width), f32),
                pltpu.VMEM((4, *square), f32),
                pltpu.VMEM((2, powers, *square), bf16),
                pltpu.VMEM((2, powers, *square), bf16),
                pltpu.VMEM(square, bf16),
                pltpu.VMEM(square, bf16),
                pltpu.VMEM((powers - 1, *square), f32),
                pltpu.VMEM((powers - 1, *square), f32),
                pltpu.VMEM((nc, steps, width), f32),
                pltpu.VMEM((nc, steps, width), f32),
                pltpu.VMEM((nx, steps, width), f32),
                pltpu.VMEM((nz, 1, width), f32),
                pltpu.VMEM((nz, 1, width), f32),
                pltpu.VMEM((total, 1), f32),
                pltpu.VMEM((total, width), f32),
                pltpu.VMEM((total, width), f32),
                pltpu.VMEM((nx, steps, width), f32),
                pltpu.VMEM((nx, steps, width), f32),
                pltpu.VMEM((nx, steps, width), f32),
                pltpu.VMEM((blocks, steps, BLOCK), f32),
                pltpu.VMEM((blocks, steps, BLOCK), f32),
                pltpu.VMEM((nc, steps, BLOCK), f32),
                pltpu.VMEM((nc, steps, BLOCK), f32),
                dma((10,)),
                dma((nc,)), dma((nc,)),
                dma((nx,)), dma((nx,)),
                dma((nz,)), dma((nz,)),
                dma((nz,)), dma((nz,)),
                dma((nc,)), dma((nc,)),
                dma((nc,)), dma((nc,)),
                dma((powers,)), dma((powers,)),
                pltpu.SemaphoreType.REGULAR((2,)),
            ],
            compiler_params=pltpu.CompilerParams(
                collective_id=0, has_side_effects=True, vmem_limit_bytes=LIMIT
            ),
        )(
            observations, obs_matrix, block_pattern, noise_precision.reshape(1, channels),
            retention, prior_mean.reshape(1, width),
            filter_matrix, filter_gain, transition, smoother_gain,
        )
        odd = lax.rem(lax.axis_index("chan"), 2) == 1
        half = BLOCK // 2
        return tuple(jnp.where(odd, array[:, :, half:], array[:, :, :half]) for array in both)

    placed = (
        P(None, "tm", "chan"), P("chan", None), P("chan", None), P("chan"),
        P(), P(), P(), P(), P(), P(),
    )
    return jax.shard_map(
        per_device,
        mesh=mesh,
        in_specs=placed,
        out_specs=(P(None, "tm", "chan"), P(None, "tm", "chan")),
        check_vma=False,
    )


def solution(mesh):
    return build(mesh, PLANE)
```

```python
import functools

import jax
import jax.numpy as jnp
from jax import lax
from jax.experimental import pallas as pl
from jax.experimental.pallas import tpu as pltpu
from jax.sharding import PartitionSpec as P

BLOCK = 128
PLANE = 4
NEAR = 2
LIMIT = 63 * 1024 * 1024
MESH = pl.DeviceIdType.MESH
f32 = jnp.float32
bf16 = jnp.bfloat16


def dot(a, b):
    return jnp.dot(a, b, preferred_element_type=f32)


def split(x):
    high = x.astype(bf16)
    return high, (x - high.astype(f32)).astype(bf16)


def times(x, high, low):
    rows = x.shape[0]
    if rows % 16:
        x_high = x.astype(bf16).astype(f32)
        both = jnp.concatenate([x_high, x - x_high], 0).astype(bf16)
        first, second = dot(both, high), dot(both, low)
        return first[:rows] + (first[rows:] + second[:rows])
    x_high, x_low = split(x)
    if rows >= 256:
        return dot(x_high, high) + (dot(x_low, high) + dot(x_high, low))
    first = dot(jnp.concatenate([x_high, x_low], 0), high)
    return first[:rows] + (first[rows:] + dot(x_high, low))


def shifted(x, distance):
    return jnp.roll(x, distance, axis=0)


def kernel(
    nx, nz, nc, steps, width, channels,
    obs_hbm, mat_hbm, pattern_hbm, noise_hbm, retention_hbm, prior_hbm, f_hbm, k_hbm, t_hbm, g_hbm,
    filtered, smoothed,
    obs, mat, pattern, noise, retention, prior, raw, fgh, fgl, wh, wl,
    own_power, other_power, part, part_in, drive, ends, starts, rho, rows_y, rows_c, fbuf, cbuf, bbuf,
    out_f, out_s, in_f, in_s,
    load_sem, rs_send, rs_recv, x_send, x_recv, e_send, e_recv, b_send, b_recv,
    of_send, of_recv, os_send, os_recv, pow_send, pow_recv, ready,
):
    tm, chan = lax.axis_index("tm"), lax.axis_index("chan")
    z, x = tm // nx, tm % nx
    span = nx * steps
    total = nz * span
    local_bits = span.bit_length() - 1
    z_bits = nz.bit_length() - 1

    loads = [
        pltpu.make_async_copy(source, target, load_sem.at[i])
        for i, (source, target) in enumerate(
            (
                (obs_hbm, obs),
                (mat_hbm, mat),
                (pattern_hbm, pattern),
                (noise_hbm, noise),
                (k_hbm, raw.at[1]),
                (f_hbm, raw.at[0]),
                (g_hbm, raw.at[2]),
                (t_hbm, raw.at[3]),
                (retention_hbm, retention),
                (prior_hbm, prior),
            )
        )
    ]
    for load in loads:
        load.start()

    def chan_peer(i):
        return {"chan": lax.rem(chan + i, nc)}

    def x_peer(i):
        return {"tm": z * nx + lax.rem(x + i, nx)}

    def z_peer(i):
        return {"tm": lax.rem(z + i, nz) * nx + x}

    near = [i for i in range(1, nz) if min(i, nz - i) <= NEAR]
    barrier = pltpu.get_barrier_semaphore()
    for i in range(1, nc):
        pl.semaphore_signal(barrier, inc=1, device_id=chan_peer(i), device_id_type=MESH)

    for i in range(1, nx):
        pl.semaphore_signal(barrier, inc=1, device_id=x_peer(i), device_id_type=MESH)
    for i in near:
        pl.semaphore_signal(barrier, inc=1, device_id=z_peer(i), device_id_type=MESH)

    def ring(distance):
        return sorted({i for i in (distance, nz - distance) if 0 < i < nz})

    rounds = [d for d in (NEAR, 2 * NEAR) if 2 * d <= nz // 2]

    def widen(k):
        for i in ring(rounds[k]):
            pl.semaphore_signal(ready.at[k], inc=1, device_id=z_peer(i), device_id_type=MESH)

    def widened(k):
        pl.semaphore_wait(ready.at[k], len(ring(rounds[k])))

    sent = []

    def landed(copies):
        for copy in reversed(copies):
            copy.wait_recv()
        sent.extend(copies)

    def far_first(count):
        return sorted(range(1, count), key=lambda i: -min(i, count - i))

    def remote(source, target, send, recv, peer):
        return pltpu.make_async_remote_copy(
            src_ref=source, dst_ref=target, send_sem=send, recv_sem=recv,
            device_id=peer, device_id_type=MESH,
        )

    fh, fl, gh, gl = fgh.at[0], fgl.at[0], fgh.at[1], fgl.at[1]
    core = lax.rem(chan, 2)
    twin = {"chan": chan + 1 - 2 * core}

    def power_copy(i):
        return remote(own_power.at[i], other_power.at[i], pow_send.at[i], pow_recv.at[i], twin)

    def square(first, last):
        def body(i, _):
            a, b = fgh[core, i], fgl[core, i]
            product = dot(a, a) + (dot(a, b) + dot(b, a))
            own_power[i] = product
            power_copy(i).start()
            h, l = split(product)
            fgh[core, i + 1] = h
            fgl[core, i + 1] = l
            return 0

        lax.fori_loop(first, last, body, 0)

    def take_powers(first, last):
        def body(i, _):
            power_copy(i).wait_recv()
            h, l = split(other_power[i])
            fgh[1 - core, i + 1] = h
            fgl[1 - core, i + 1] = l
            return 0

        lax.fori_loop(first, last, body, 0)

    for load in loads[:4]:
        load.wait()
    weighted = obs[...].astype(f32) * noise[...].reshape(1, 1, channels)
    weighted = weighted.reshape(nc * steps, channels).astype(bf16)
    lane_block = lax.broadcasted_iota(jnp.int32, (BLOCK, width), 1) // BLOCK
    used = []
    for i in range(channels // BLOCK):
        mask = jnp.zeros((BLOCK, width), f32)
        for j in range(width // BLOCK):
            mask = jnp.where(lane_block == j, pattern[i, j].astype(f32), mask)
        used.append(mat[i * BLOCK : (i + 1) * BLOCK] * mask.astype(bf16))
    information = dot(weighted, jnp.concatenate(used, 0))

    loads[4].wait()
    kh, kl = split(raw[1])
    part[...] = times(information, kh, kl).reshape(nc, steps, width)


    pl.semaphore_wait(barrier, len(near) + nx + nc - 2)
    sums = []
    for i in far_first(nc):
        there = lax.rem(chan + i, nc)
        copy = remote(part.at[there], part_in.at[chan], rs_send.at[i], rs_recv.at[i], chan_peer(i))
        copy.start()
        sums.append(copy)
    part_in[chan] = part[chan]
    if rounds:
        widen(0)
    loads[5].wait()
    loads[6].wait()
    fgh[core, 0], fgl[core, 0] = split(raw[2 * core])
    square(0, 3)

    loads[8].wait()
    loads[9].wait()
    row = retention[pl.ds(chan, 1), :]
    index = lax.broadcasted_iota(jnp.int32, (total, 1), 0)
    plane, rest = index % nz, index // nz
    wanted = plane * span + (rest % nx) * steps + rest // nx
    there = lax.broadcasted_iota(jnp.int32, (total, total), 1)
    column = jnp.sum(jnp.where(there == wanted, row, 0.0), axis=1, keepdims=True)

    def rows_of(t):
        start = ((t % steps) * nx + t // steps) * nz
        return slice(start, start + nz)

    running = column[:nz]
    rho[:nz] = running
    for t in range(1, span):
        running = running * column[rows_of(t)]
        rho[rows_of(t)] = running
    block_row = lax.broadcasted_iota(jnp.int32, (nz, 1), 0)
    chain = jnp.where(block_row >= 1, shifted(running, 1), 0.0)
    block_factors = [chain]
    for level in range(1, z_bits):
        chain = chain * shifted(chain, 1 << (level - 1))
        block_factors.append(jnp.where(block_row >= (1 << level), chain, 0.0))
    step_row = lax.broadcasted_iota(jnp.int32, (span, 1), 0)
    here = lax.broadcasted_iota(jnp.int32, (span, total), 0)
    there = lax.broadcasted_iota(jnp.int32, (span, total), 1)
    own = jnp.sum(jnp.where(there == here + z * span, row, 0.0), axis=1, keepdims=True)
    own_factors = [jnp.where(step_row >= 1, own, 0.0)]
    for level in range(1, local_bits):
        own = own * shifted(own, 1 << (level - 1))
        own_factors.append(jnp.where(step_row >= (1 << level), own, 0.0))


    landed(sums)
    driving = part_in[0]
    for i in range(1, nc):
        driving = driving + part_in[i]
    drive[x] = driving
    spread = []
    for i in far_first(nx):
        copy = remote(drive.at[x], drive.at[x], x_send.at[i], x_recv.at[i], x_peer(i))
        copy.start()
        spread.append(copy)

    if rounds:
        widened(0)
    if len(rounds) > 1:
        widen(1)
    square(3, 4)
    fgh[1 - core, 0], fgl[1 - core, 0] = split(raw[2 * (1 - core)])
    loads[7].wait()
    th, tl = split(raw[3])
    eye = lax.broadcasted_iota(jnp.int32, (width, width), 0) == lax.broadcasted_iota(
        jnp.int32, (width, width), 1
    )
    product = dot(th, gh[0]) + (dot(th, gl[0]) + dot(tl, gh[0]))
    wh[...], wl[...] = split(jnp.where(eye, 1.0, 0.0) - product)
    take_powers(0, 4)

    landed(spread)
    if len(rounds) > 1:
        widened(1)

    local = drive[...].reshape(span, width)
    for level in range(local_bits):
        moved = shifted(local, 1 << level)
        local = local + own_factors[level] * times(moved, fh[level], fl[level])
    ends[z] = local[span - 1 :]
    fbuf[...] = local.reshape(nx, steps, width)
    across = []
    for i in far_first(nz):
        copy = remote(ends.at[z], ends.at[z], e_send.at[i], e_recv.at[i], z_peer(i))
        copy.start()
        across.append(copy)

    square(4, local_bits + z_bits - 2)

    last_plane = z == nz - 1
    corrected = times(local, wh[...], wl[...])
    corrected = jnp.where(last_plane & (step_row == span - 1), local, corrected)
    cbuf[...] = corrected.reshape(nx, steps, width)
    backward = corrected
    for level in (2, 1, 0):
        backward = backward + times(shifted(backward, -(1 << level)), gh[level], gl[level])
    bbuf[...] = backward.reshape(nx, steps, width)
    for level in range(local_bits - 1, 2, -1):
        backward = backward + times(shifted(backward, -(1 << level)), gh[level], gl[level])
    starts[z] = backward[:1]
    for i in far_first(nz):
        copy = remote(starts.at[z], starts.at[z], b_send.at[i], b_recv.at[i], z_peer(i))
        copy.start()
        across.append(copy)

    square(local_bits + z_bits - 2, local_bits + z_bits - 1)
    take_powers(4, local_bits + z_bits - 2)

    landed(across[: nz - 1])

    carry = jnp.where(block_row == 0, prior[...], shifted(ends[...].reshape(nz, width), 1))
    for level in range(z_bits):
        if level == z_bits - 1:
            take_powers(local_bits + z_bits - 2, local_bits + z_bits - 1)
        moved = shifted(carry, 1 << level)
        high, low = fh[local_bits + level], fl[local_bits + level]
        carry = carry + block_factors[level] * times(moved, high, low)

    rows_y[:nz] = times(carry, fh[0], fl[0])
    count = nz
    for level in (*range(3, local_bits), 0, 1, 2):
        rows_y[count : 2 * count] = times(rows_y[:count], fh[level], fl[level])
        count = 2 * count
    rows_y[...] = rows_y[...] * rho[...]

    def own_rows(rows):
        return jnp.concatenate([rows[pl.ds((p * nx + x) * nz + z, 1), :] for p in range(steps)], 0)

    def send_out(state, out, into, send, recv):
        copies = []
        for k in range(width // BLOCK):
            out[k] = state[:, k * BLOCK : (k + 1) * BLOCK]
        for i in far_first(nc):
            there = lax.rem(chan + i, nc)
            copy = remote(out.at[there // 2], into.at[chan], send.at[i], recv.at[i], chan_peer(i))
            copy.start()
            copies.append(copy)
        into[chan] = out[chan // 2]
        return copies


    rows_c[...] = times(rows_y[...], wh[...], wl[...])
    rows_c[total - 1 :] = rows_y[total - 1 :]
    own_corrected = cbuf[x] + own_rows(rows_c)

    for level in (2, 1, 0):
        half = nx * nz << level
        rows_c[:half] = rows_c[:half] + times(rows_c[half : 2 * half], gh[level], gl[level])

    copies_f = send_out(fbuf[x] + own_rows(rows_y), out_f, in_f, of_send, of_recv)
    landed(across[nz - 1 :])
    whole = block_row == z
    for q in range(nx):
        own_start = bbuf[q][:1]
        if q == 0:
            extra = jnp.where(whole, own_start, starts[...].reshape(nz, width))
        else:
            extra = jnp.where(whole, own_start, 0.0)
        value = rows_c[q * nz : (q + 1) * nz] + extra
        rows_y[q * nz : (q + 1) * nz] = value
        later = jnp.where(block_row < nz - 1, shifted(value, -1), 0.0)
        rows_y[(nx + q) * nz : (nx + q + 1) * nz] = later
    first = pl.multiple_of((1 + x) * nz, nz)
    tail = rows_y[pl.ds(first, nx * nz), :]
    for level in range(local_bits - 1, 2, -1):
        half = nz << (level - 3)
        tail = tail[:half] + times(tail[half:], gh[level], gl[level])
    for level in range(z_bits):
        distance = 1 << level
        moved = jnp.where(block_row < nz - distance, shifted(tail, -distance), 0.0)
        high, low = gh[local_bits + level], gl[local_bits + level]
        tail = tail + times(moved, high, low)
    after = jnp.sum(jnp.where(whole, tail, 0.0), axis=0, keepdims=True)

    row8 = lax.broadcasted_iota(jnp.int32, (steps, 1), 0)
    placed = jnp.where(row8 == steps - 1, after, 0.0)
    state = own_corrected + times(placed, gh[0], gl[0])
    for level in range(3):
        distance = 1 << level
        moved = jnp.where(row8 < steps - distance, shifted(state, -distance), 0.0)
        state = state + times(moved, gh[level], gl[level])
    copies_s = send_out(state, out_s, in_s, os_send, os_recv)

    for copy in sent + copies_f + copies_s:
        copy.wait_send()
    for i in range(local_bits + z_bits - 1):
        power_copy(i).wait_send()
    for copies, into, result in ((copies_f, in_f, filtered), (copies_s, in_s, smoothed)):
        landed(copies)
        result[...] = into[...]


def build(mesh, nx):
    nc = mesh.shape["chan"]
    nz = mesh.shape["tm"] // nx

    def per_device(
        observations, obs_matrix, block_pattern, noise_precision, retention, prior_mean,
        filter_matrix, filter_gain, transition, smoother_gain,
    ):
        series, steps, channels = observations.shape
        width = obs_matrix.shape[1]
        span = nx * steps
        total = span * nz
        powers = total.bit_length() - 1
        vmem = pl.BlockSpec(memory_space=pltpu.VMEM)
        hbm = pl.BlockSpec(memory_space=pl.ANY)
        dma = pltpu.SemaphoreType.DMA
        square = (width, width)
        blocks = width // BLOCK
        result = jax.ShapeDtypeStruct((series, steps, BLOCK), f32)
        both = pl.pallas_call(
            functools.partial(kernel, nx, nz, nc, steps, width, channels),
            out_shape=(result, result),
            in_specs=[hbm] * 10,
            out_specs=(vmem, vmem),
            scratch_shapes=[
                pltpu.VMEM((series, steps, channels), bf16),
                pltpu.VMEM((channels, width), bf16),
                pltpu.SMEM((channels // BLOCK, width // BLOCK), jnp.int32),
                pltpu.VMEM((1, channels), f32),
                pltpu.VMEM((series, total), f32),
                pltpu.VMEM((1, width), f32),
                pltpu.VMEM((4, *square), f32),
                pltpu.VMEM((2, powers, *square), bf16),
                pltpu.VMEM((2, powers, *square), bf16),
                pltpu.VMEM(square, bf16),
                pltpu.VMEM(square, bf16),
                pltpu.VMEM((powers - 1, *square), f32),
                pltpu.VMEM((powers - 1, *square), f32),
                pltpu.VMEM((nc, steps, width), f32),
                pltpu.VMEM((nc, steps, width), f32),
                pltpu.VMEM((nx, steps, width), f32),
                pltpu.VMEM((nz, 1, width), f32),
                pltpu.VMEM((nz, 1, width), f32),
                pltpu.VMEM((total, 1), f32),
                pltpu.VMEM((total, width), f32),
                pltpu.VMEM((total, width), f32),
                pltpu.VMEM((nx, steps, width), f32),
                pltpu.VMEM((nx, steps, width), f32),
                pltpu.VMEM((nx, steps, width), f32),
                pltpu.VMEM((blocks, steps, BLOCK), f32),
                pltpu.VMEM((blocks, steps, BLOCK), f32),
                pltpu.VMEM((nc, steps, BLOCK), f32),
                pltpu.VMEM((nc, steps, BLOCK), f32),
                dma((10,)),
                dma((nc,)), dma((nc,)),
                dma((nx,)), dma((nx,)),
                dma((nz,)), dma((nz,)),
                dma((nz,)), dma((nz,)),
                dma((nc,)), dma((nc,)),
                dma((nc,)), dma((nc,)),
                dma((powers,)), dma((powers,)),
                pltpu.SemaphoreType.REGULAR((2,)),
            ],
            compiler_params=pltpu.CompilerParams(
                collective_id=0, has_side_effects=True, vmem_limit_bytes=LIMIT
            ),
        )(
            observations, obs_matrix, block_pattern, noise_precision.reshape(1, channels),
            retention, prior_mean.reshape(1, width),
            filter_matrix, filter_gain, transition, smoother_gain,
        )
        odd = lax.rem(lax.axis_index("chan"), 2) == 1
        half = BLOCK // 2
        return tuple(jnp.where(odd, array[:, :, half:], array[:, :, :half]) for array in both)

    placed = (
        P(None, "tm", "chan"), P("chan", None), P("chan", None), P("chan"),
        P(), P(), P(), P(), P(), P(),
    )
    return jax.shard_map(
        per_device,
        mesh=mesh,
        in_specs=placed,
        out_specs=(P(None, "tm", "chan"), P(None, "tm", "chan")),
        check_vma=False,
    )


def solution(mesh):
    return build(mesh, PLANE)
```

```python
import functools

import jax
import jax.numpy as jnp
from jax import lax
from jax.experimental import pallas as pl
from jax.experimental.pallas import tpu as pltpu
from jax.sharding import PartitionSpec as P

BLOCK = 128
PLANE = 4
NEAR = 2
LIMIT = 63 * 1024 * 1024
MESH = pl.DeviceIdType.MESH
f32 = jnp.float32
bf16 = jnp.bfloat16


def dot(a, b):
    return jnp.dot(a, b, preferred_element_type=f32)


def split(x):
    high = x.astype(bf16)
    return high, (x - high.astype(f32)).astype(bf16)


def times(x, high, low):
    rows = x.shape[0]
    if rows % 16:
        x_high = x.astype(bf16).astype(f32)
        both = jnp.concatenate([x_high, x - x_high], 0).astype(bf16)
        first, second = dot(both, high), dot(both, low)
        return first[:rows] + (first[rows:] + second[:rows])
    x_high, x_low = split(x)
    if rows >= 256:
        return dot(x_high, high) + (dot(x_low, high) + dot(x_high, low))
    first = dot(jnp.concatenate([x_high, x_low], 0), high)
    return first[:rows] + (first[rows:] + dot(x_high, low))


def shifted(x, distance):
    return jnp.roll(x, distance, axis=0)


def kernel(
    nx, nz, nc, steps, width, channels,
    obs_hbm, mat_hbm, pattern_hbm, noise_hbm, retention_hbm, prior_hbm, f_hbm, k_hbm, t_hbm, g_hbm,
    filtered, smoothed,
    obs, mat, pattern, noise, retention, prior, raw, fgh, fgl, wh, wl,
    own_power, other_power, part, part_in, drive, ends, starts, rho, rows_y, rows_c, fbuf, cbuf, bbuf,
    out_f, out_s, in_f, in_s,
    load_sem, rs_send, rs_recv, x_send, x_recv, e_send, e_recv, b_send, b_recv,
    of_send, of_recv, os_send, os_recv, pow_send, pow_recv, ready,
):
    tm, chan = lax.axis_index("tm"), lax.axis_index("chan")
    z, x = tm // nx, tm % nx
    span = nx * steps
    total = nz * span
    local_bits = span.bit_length() - 1
    z_bits = nz.bit_length() - 1

    loads = [
        pltpu.make_async_copy(source, target, load_sem.at[i])
        for i, (source, target) in enumerate(
            (
                (obs_hbm, obs),
                (mat_hbm, mat),
                (pattern_hbm, pattern),
                (noise_hbm, noise),
                (k_hbm, raw.at[1]),
                (f_hbm, raw.at[0]),
                (g_hbm, raw.at[2]),
                (t_hbm, raw.at[3]),
                (retention_hbm, retention),
                (prior_hbm, prior),
            )
        )
    ]
    for load in loads:
        load.start()

    def chan_peer(i):
        return {"chan": lax.rem(chan + i, nc)}

    def x_peer(i):
        return {"tm": z * nx + lax.rem(x + i, nx)}

    def z_peer(i):
        return {"tm": lax.rem(z + i, nz) * nx + x}

    near = [i for i in range(1, nz) if min(i, nz - i) <= NEAR]
    barrier = pltpu.get_barrier_semaphore()
    for i in range(1, nc):
        pl.semaphore_signal(barrier, inc=1, device_id=chan_peer(i), device_id_type=MESH)

    for i in range(1, nx):
        pl.semaphore_signal(barrier, inc=1, device_id=x_peer(i), device_id_type=MESH)
    for i in near:
        pl.semaphore_signal(barrier, inc=1, device_id=z_peer(i), device_id_type=MESH)

    def ring(distance):
        return sorted({i for i in (distance, nz - distance) if 0 < i < nz})

    rounds = [d for d in (NEAR, 2 * NEAR) if 2 * d <= nz // 2]

    def widen(k):
        for i in ring(rounds[k]):
            pl.semaphore_signal(ready.at[k], inc=1, device_id=z_peer(i), device_id_type=MESH)

    def widened(k):
        pl.semaphore_wait(ready.at[k], len(ring(rounds[k])))

    sent = []

    def landed(copies):
        for copy in reversed(copies):
            copy.wait_recv()
        sent.extend(copies)

    def far_first(count):
        return sorted(range(1, count), key=lambda i: -min(i, count - i))

    def remote(source, target, send, recv, peer):
        return pltpu.make_async_remote_copy(
            src_ref=source, dst_ref=target, send_sem=send, recv_sem=recv,
            device_id=peer, device_id_type=MESH,
        )

    fh, fl, gh, gl = fgh.at[0], fgl.at[0], fgh.at[1], fgl.at[1]
    core = lax.rem(chan, 2)
    twin = {"chan": chan + 1 - 2 * core}

    def power_copy(i):
        return remote(own_power.at[i], other_power.at[i], pow_send.at[i], pow_recv.at[i], twin)

    def square(first, last):
        def body(i, _):
            a, b = fgh[core, i], fgl[core, i]
            product = dot(a, a) + (dot(a, b) + dot(b, a))
            own_power[i] = product
            power_copy(i).start()
            h, l = split(product)
            fgh[core, i + 1] = h
            fgl[core, i + 1] = l
            return 0

        lax.fori_loop(first, last, body, 0)

    def take_powers(first, last):
        def body(i, _):
            power_copy(i).wait_recv()
            h, l = split(other_power[i])
            fgh[1 - core, i + 1] = h
            fgl[1 - core, i + 1] = l
            return 0

        lax.fori_loop(first, last, body, 0)

    for load in loads[:4]:
        load.wait()
    weighted = obs[...].astype(f32) * noise[...].reshape(1, 1, channels)
    weighted = weighted.reshape(nc * steps, channels).astype(bf16)
    lane_block = lax.broadcasted_iota(jnp.int32, (BLOCK, width), 1) // BLOCK
    used = []
    for i in range(channels // BLOCK):
        mask = jnp.zeros((BLOCK, width), f32)
        for j in range(width // BLOCK):
            mask = jnp.where(lane_block == j, pattern[i, j].astype(f32), mask)
        used.append(mat[i * BLOCK : (i + 1) * BLOCK] * mask.astype(bf16))
    information = dot(weighted, jnp.concatenate(used, 0))

    loads[4].wait()
    kh, kl = split(raw[1])
    part[...] = times(information, kh, kl).reshape(nc, steps, width)


    pl.semaphore_wait(barrier, len(near) + nx + nc - 2)
    sums = []
    for i in far_first(nc):
        there = lax.rem(chan + i, nc)
        copy = remote(part.at[there], part_in.at[chan], rs_send.at[i], rs_recv.at[i], chan_peer(i))
        copy.start()
        sums.append(copy)
    part_in[chan] = part[chan]
    if rounds:
        widen(0)
    loads[5].wait()
    loads[6].wait()
    fgh[core, 0], fgl[core, 0] = split(raw[2 * core])
    square(0, 3)

    loads[8].wait()
    loads[9].wait()
    row = retention[pl.ds(chan, 1), :]
    index = lax.broadcasted_iota(jnp.int32, (total, 1), 0)
    plane, rest = index % nz, index // nz
    wanted = plane * span + (rest % nx) * steps + rest // nx
    there = lax.broadcasted_iota(jnp.int32, (total, total), 1)
    column = jnp.sum(jnp.where(there == wanted, row, 0.0), axis=1, keepdims=True)

    def rows_of(t):
        start = ((t % steps) * nx + t // steps) * nz
        return slice(start, start + nz)

    running = column[:nz]
    rho[:nz] = running
    for t in range(1, span):
        running = running * column[rows_of(t)]
        rho[rows_of(t)] = running
    block_row = lax.broadcasted_iota(jnp.int32, (nz, 1), 0)
    chain = jnp.where(block_row >= 1, shifted(running, 1), 0.0)
    block_factors = [chain]
    for level in range(1, z_bits):
        chain = chain * shifted(chain, 1 << (level - 1))
        block_factors.append(jnp.where(block_row >= (1 << level), chain, 0.0))
    step_row = lax.broadcasted_iota(jnp.int32, (span, 1), 0)
    here = lax.broadcasted_iota(jnp.int32, (span, total), 0)
    there = lax.broadcasted_iota(jnp.int32, (span, total), 1)
    own = jnp.sum(jnp.where(there == here + z * span, row, 0.0), axis=1, keepdims=True)
    own_factors = [jnp.where(step_row >= 1, own, 0.0)]
    for level in range(1, local_bits):
        own = own * shifted(own, 1 << (level - 1))
        own_factors.append(jnp.where(step_row >= (1 << level), own, 0.0))


    landed(sums)
    driving = part_in[0]
    for i in range(1, nc):
        driving = driving + part_in[i]
    drive[x] = driving
    spread = []
    for i in far_first(nx):
        copy = remote(drive.at[x], drive.at[x], x_send.at[i], x_recv.at[i], x_peer(i))
        copy.start()
        spread.append(copy)

    if rounds:
        widened(0)
    if len(rounds) > 1:
        widen(1)
    square(3, 4)
    fgh[1 - core, 0], fgl[1 - core, 0] = split(raw[2 * (1 - core)])
    loads[7].wait()
    th, tl = split(raw[3])
    eye = lax.broadcasted_iota(jnp.int32, (width, width), 0) == lax.broadcasted_iota(
        jnp.int32, (width, width), 1
    )
    product = dot(th, gh[0]) + (dot(th, gl[0]) + dot(tl, gh[0]))
    wh[...], wl[...] = split(jnp.where(eye, 1.0, 0.0) - product)
    take_powers(0, local_bits - 2)

    landed(spread)
    if len(rounds) > 1:
        widened(1)

    local = drive[...].reshape(span, width)
    for level in range(local_bits):
        if level == local_bits - 1:
            take_powers(local_bits - 2, local_bits - 1)
        moved = shifted(local, 1 << level)
        local = local + own_factors[level] * times(moved, fh[level], fl[level])
    ends[z] = local[span - 1 :]
    fbuf[...] = local.reshape(nx, steps, width)
    across = []
    for i in far_first(nz):
        copy = remote(ends.at[z], ends.at[z], e_send.at[i], e_recv.at[i], z_peer(i))
        copy.start()
        across.append(copy)

    square(4, local_bits + z_bits - 2)

    last_plane = z == nz - 1
    corrected = times(local, wh[...], wl[...])
    corrected = jnp.where(last_plane & (step_row == span - 1), local, corrected)
    cbuf[...] = corrected.reshape(nx, steps, width)
    backward = corrected
    for level in (2, 1, 0):
        backward = backward + times(shifted(backward, -(1 << level)), gh[level], gl[level])
    bbuf[...] = backward.reshape(nx, steps, width)
    for level in range(local_bits - 1, 2, -1):
        backward = backward + times(shifted(backward, -(1 << level)), gh[level], gl[level])
    starts[z] = backward[:1]
    for i in far_first(nz):
        copy = remote(starts.at[z], starts.at[z], b_send.at[i], b_recv.at[i], z_peer(i))
        copy.start()
        across.append(copy)

    square(local_bits + z_bits - 2, local_bits + z_bits - 1)
    take_powers(local_bits - 1, local_bits + z_bits - 2)

    landed(across[: nz - 1])

    carry = jnp.where(block_row == 0, prior[...], shifted(ends[...].reshape(nz, width), 1))
    for level in range(z_bits):
        if level == z_bits - 1:
            take_powers(local_bits + z_bits - 2, local_bits + z_bits - 1)
        moved = shifted(carry, 1 << level)
        high, low = fh[local_bits + level], fl[local_bits + level]
        carry = carry + block_factors[level] * times(moved, high, low)

    rows_y[:nz] = times(carry, fh[0], fl[0])
    count = nz
    for level in (*range(3, local_bits), 0, 1, 2):
        rows_y[count : 2 * count] = times(rows_y[:count], fh[level], fl[level])
        count = 2 * count
    rows_y[...] = rows_y[...] * rho[...]

    def own_rows(rows):
        return jnp.concatenate([rows[pl.ds((p * nx + x) * nz + z, 1), :] for p in range(steps)], 0)

    def send_out(state, out, into, send, recv):
        copies = []
        for k in range(width // BLOCK):
            out[k] = state[:, k * BLOCK : (k + 1) * BLOCK]
        for i in far_first(nc):
            there = lax.rem(chan + i, nc)
            copy = remote(out.at[there // 2], into.at[chan], send.at[i], recv.at[i], chan_peer(i))
            copy.start()
            copies.append(copy)
        into[chan] = out[chan // 2]
        return copies


    rows_c[...] = times(rows_y[...], wh[...], wl[...])
    rows_c[total - 1 :] = rows_y[total - 1 :]
    own_corrected = cbuf[x] + own_rows(rows_c)

    for level in (2, 1, 0):
        half = nx * nz << level
        rows_c[:half] = rows_c[:half] + times(rows_c[half : 2 * half], gh[level], gl[level])

    copies_f = send_out(fbuf[x] + own_rows(rows_y), out_f, in_f, of_send, of_recv)
    landed(across[nz - 1 :])
    whole = block_row == z
    for q in range(nx):
        own_start = bbuf[q][:1]
        if q == 0:
            extra = jnp.where(whole, own_start, starts[...].reshape(nz, width))
        else:
            extra = jnp.where(whole, own_start, 0.0)
        value = rows_c[q * nz : (q + 1) * nz] + extra
        rows_y[q * nz : (q + 1) * nz] = value
        later = jnp.where(block_row < nz - 1, shifted(value, -1), 0.0)
        rows_y[(nx + q) * nz : (nx + q + 1) * nz] = later
    first = pl.multiple_of((1 + x) * nz, nz)
    tail = rows_y[pl.ds(first, nx * nz), :]
    for level in range(local_bits - 1, 2, -1):
        half = nz << (level - 3)
        tail = tail[:half] + times(tail[half:], gh[level], gl[level])
    for level in range(z_bits):
        distance = 1 << level
        moved = jnp.where(block_row < nz - distance, shifted(tail, -distance), 0.0)
        high, low = gh[local_bits + level], gl[local_bits + level]
        tail = tail + times(moved, high, low)
    after = jnp.sum(jnp.where(whole, tail, 0.0), axis=0, keepdims=True)

    row8 = lax.broadcasted_iota(jnp.int32, (steps, 1), 0)
    placed = jnp.where(row8 == steps - 1, after, 0.0)
    state = own_corrected + times(placed, gh[0], gl[0])
    for level in range(3):
        distance = 1 << level
        moved = jnp.where(row8 < steps - distance, shifted(state, -distance), 0.0)
        state = state + times(moved, gh[level], gl[level])
    copies_s = send_out(state, out_s, in_s, os_send, os_recv)

    for copy in sent + copies_f + copies_s:
        copy.wait_send()
    for i in range(local_bits + z_bits - 1):
        power_copy(i).wait_send()
    for copies, into, result in ((copies_f, in_f, filtered), (copies_s, in_s, smoothed)):
        landed(copies)
        result[...] = into[...]


def build(mesh, nx):
    nc = mesh.shape["chan"]
    nz = mesh.shape["tm"] // nx

    def per_device(
        observations, obs_matrix, block_pattern, noise_precision, retention, prior_mean,
        filter_matrix, filter_gain, transition, smoother_gain,
    ):
        series, steps, channels = observations.shape
        width = obs_matrix.shape[1]
        span = nx * steps
        total = span * nz
        powers = total.bit_length() - 1
        vmem = pl.BlockSpec(memory_space=pltpu.VMEM)
        hbm = pl.BlockSpec(memory_space=pl.ANY)
        dma = pltpu.SemaphoreType.DMA
        square = (width, width)
        blocks = width // BLOCK
        result = jax.ShapeDtypeStruct((series, steps, BLOCK), f32)
        both = pl.pallas_call(
            functools.partial(kernel, nx, nz, nc, steps, width, channels),
            out_shape=(result, result),
            in_specs=[hbm] * 10,
            out_specs=(vmem, vmem),
            scratch_shapes=[
                pltpu.VMEM((series, steps, channels), bf16),
                pltpu.VMEM((channels, width), bf16),
                pltpu.SMEM((channels // BLOCK, width // BLOCK), jnp.int32),
                pltpu.VMEM((1, channels), f32),
                pltpu.VMEM((series, total), f32),
                pltpu.VMEM((1, width), f32),
                pltpu.VMEM((4, *square), f32),
                pltpu.VMEM((2, powers, *square), bf16),
                pltpu.VMEM((2, powers, *square), bf16),
                pltpu.VMEM(square, bf16),
                pltpu.VMEM(square, bf16),
                pltpu.VMEM((powers - 1, *square), f32),
                pltpu.VMEM((powers - 1, *square), f32),
                pltpu.VMEM((nc, steps, width), f32),
                pltpu.VMEM((nc, steps, width), f32),
                pltpu.VMEM((nx, steps, width), f32),
                pltpu.VMEM((nz, 1, width), f32),
                pltpu.VMEM((nz, 1, width), f32),
                pltpu.VMEM((total, 1), f32),
                pltpu.VMEM((total, width), f32),
                pltpu.VMEM((total, width), f32),
                pltpu.VMEM((nx, steps, width), f32),
                pltpu.VMEM((nx, steps, width), f32),
                pltpu.VMEM((nx, steps, width), f32),
                pltpu.VMEM((blocks, steps, BLOCK), f32),
                pltpu.VMEM((blocks, steps, BLOCK), f32),
                pltpu.VMEM((nc, steps, BLOCK), f32),
                pltpu.VMEM((nc, steps, BLOCK), f32),
                dma((10,)),
                dma((nc,)), dma((nc,)),
                dma((nx,)), dma((nx,)),
                dma((nz,)), dma((nz,)),
                dma((nz,)), dma((nz,)),
                dma((nc,)), dma((nc,)),
                dma((nc,)), dma((nc,)),
                dma((powers,)), dma((powers,)),
                pltpu.SemaphoreType.REGULAR((2,)),
            ],
            compiler_params=pltpu.CompilerParams(
                collective_id=0, has_side_effects=True, vmem_limit_bytes=LIMIT
            ),
        )(
            observations, obs_matrix, block_pattern, noise_precision.reshape(1, channels),
            retention, prior_mean.reshape(1, width),
            filter_matrix, filter_gain, transition, smoother_gain,
        )
        odd = lax.rem(lax.axis_index("chan"), 2) == 1
        half = BLOCK // 2
        return tuple(jnp.where(odd, array[:, :, half:], array[:, :, :half]) for array in both)

    placed = (
        P(None, "tm", "chan"), P("chan", None), P("chan", None), P("chan"),
        P(), P(), P(), P(), P(), P(),
    )
    return jax.shard_map(
        per_device,
        mesh=mesh,
        in_specs=placed,
        out_specs=(P(None, "tm", "chan"), P(None, "tm", "chan")),
        check_vma=False,
    )


def solution(mesh):
    return build(mesh, PLANE)
```

```python
import functools

import jax
import jax.numpy as jnp
from jax import lax
from jax.experimental import pallas as pl
from jax.experimental.pallas import tpu as pltpu
from jax.sharding import PartitionSpec as P

BLOCK = 128
PLANE = 4
NEAR = 2
LIMIT = 63 * 1024 * 1024
MESH = pl.DeviceIdType.MESH
f32 = jnp.float32
bf16 = jnp.bfloat16


def dot(a, b):
    return jnp.dot(a, b, preferred_element_type=f32)


def split(x):
    high = x.astype(bf16)
    return high, (x - high.astype(f32)).astype(bf16)


def times(x, high, low):
    rows = x.shape[0]
    if rows % 16:
        x_high = x.astype(bf16).astype(f32)
        both = jnp.concatenate([x_high, x - x_high], 0).astype(bf16)
        first, second = dot(both, high), dot(both, low)
        return first[:rows] + (first[rows:] + second[:rows])
    x_high, x_low = split(x)
    if rows >= 256:
        return dot(x_high, high) + (dot(x_low, high) + dot(x_high, low))
    first = dot(jnp.concatenate([x_high, x_low], 0), high)
    return first[:rows] + (first[rows:] + dot(x_high, low))


def shifted(x, distance):
    return jnp.roll(x, distance, axis=0)


def kernel(
    nx, nz, nc, steps, width, channels,
    obs_hbm, mat_hbm, pattern_hbm, noise_hbm, retention_hbm, prior_hbm, f_hbm, k_hbm, t_hbm, g_hbm,
    filtered, smoothed,
    obs, mat, pattern, noise, retention, prior, raw, fgh, fgl, wh, wl,
    own_power, other_power, part, part_in, drive, ends, starts, rho, rows_y, rows_c, fbuf, cbuf, bbuf,
    out_f, out_s, in_f, in_s,
    load_sem, rs_send, rs_recv, x_send, x_recv, e_send, e_recv, b_send, b_recv,
    of_send, of_recv, os_send, os_recv, pow_send, pow_recv, ready,
):
    tm, chan = lax.axis_index("tm"), lax.axis_index("chan")
    z, x = tm // nx, tm % nx
    span = nx * steps
    total = nz * span
    local_bits = span.bit_length() - 1
    z_bits = nz.bit_length() - 1

    loads = [
        pltpu.make_async_copy(source, target, load_sem.at[i])
        for i, (source, target) in enumerate(
            (
                (obs_hbm, obs),
                (mat_hbm, mat),
                (pattern_hbm, pattern),
                (noise_hbm, noise),
                (k_hbm, raw.at[1]),
                (f_hbm, raw.at[0]),
                (g_hbm, raw.at[2]),
                (t_hbm, raw.at[3]),
                (retention_hbm, retention),
                (prior_hbm, prior),
            )
        )
    ]
    for load in loads:
        load.start()

    def chan_peer(i):
        return {"chan": lax.rem(chan + i, nc)}

    def x_peer(i):
        return {"tm": z * nx + lax.rem(x + i, nx)}

    def z_peer(i):
        return {"tm": lax.rem(z + i, nz) * nx + x}

    near = [i for i in range(1, nz) if min(i, nz - i) <= NEAR]
    barrier = pltpu.get_barrier_semaphore()
    for i in range(1, nc):
        pl.semaphore_signal(barrier, inc=1, device_id=chan_peer(i), device_id_type=MESH)

    for i in range(1, nx):
        pl.semaphore_signal(barrier, inc=1, device_id=x_peer(i), device_id_type=MESH)
    for i in near:
        pl.semaphore_signal(barrier, inc=1, device_id=z_peer(i), device_id_type=MESH)

    def ring(distance):
        return sorted({i for i in (distance, nz - distance) if 0 < i < nz})

    rounds = [d for d in (NEAR, 2 * NEAR) if 2 * d <= nz // 2]

    def widen(k):
        for i in ring(rounds[k]):
            pl.semaphore_signal(ready.at[k], inc=1, device_id=z_peer(i), device_id_type=MESH)

    def widened(k):
        pl.semaphore_wait(ready.at[k], len(ring(rounds[k])))

    sent = []

    def landed(copies):
        for copy in reversed(copies):
            copy.wait_recv()
        sent.extend(copies)

    def far_first(count):
        return sorted(range(1, count), key=lambda i: -min(i, count - i))

    def remote(source, target, send, recv, peer):
        return pltpu.make_async_remote_copy(
            src_ref=source, dst_ref=target, send_sem=send, recv_sem=recv,
            device_id=peer, device_id_type=MESH,
        )

    fh, fl, gh, gl = fgh.at[0], fgl.at[0], fgh.at[1], fgl.at[1]
    core = lax.rem(chan, 2)
    twin = {"chan": chan + 1 - 2 * core}

    def power_copy(i):
        return remote(own_power.at[i], other_power.at[i], pow_send.at[i], pow_recv.at[i], twin)

    def square(first, last):
        def body(i, _):
            a, b = fgh[core, i], fgl[core, i]
            product = dot(a, a) + (dot(a, b) + dot(b, a))
            own_power[i] = product
            power_copy(i).start()
            h, l = split(product)
            fgh[core, i + 1] = h
            fgl[core, i + 1] = l
            return 0

        lax.fori_loop(first, last, body, 0)

    def take_powers(first, last):
        def body(i, _):
            power_copy(i).wait_recv()
            h, l = split(other_power[i])
            fgh[1 - core, i + 1] = h
            fgl[1 - core, i + 1] = l
            return 0

        lax.fori_loop(first, last, body, 0)

    for load in loads[:4]:
        load.wait()
    weighted = obs[...].astype(f32) * noise[...].reshape(1, 1, channels)
    weighted = weighted.reshape(nc * steps, channels).astype(bf16)
    lane_block = lax.broadcasted_iota(jnp.int32, (BLOCK, width), 1) // BLOCK
    used = []
    for i in range(channels // BLOCK):
        mask = jnp.zeros((BLOCK, width), f32)
        for j in range(width // BLOCK):
            mask = jnp.where(lane_block == j, pattern[i, j].astype(f32), mask)
        used.append(mat[i * BLOCK : (i + 1) * BLOCK] * mask.astype(bf16))
    information = dot(weighted, jnp.concatenate(used, 0))

    loads[4].wait()
    kh, kl = split(raw[1])
    part[...] = times(information, kh, kl).reshape(nc, steps, width)


    pl.semaphore_wait(barrier, len(near) + nx + nc - 2)
    sums = []
    for i in far_first(nc):
        there = lax.rem(chan + i, nc)
        copy = remote(part.at[there], part_in.at[chan], rs_send.at[i], rs_recv.at[i], chan_peer(i))
        copy.start()
        sums.append(copy)
    part_in[chan] = part[chan]
    if rounds:
        widen(0)
    loads[5].wait()
    loads[6].wait()
    fgh[core, 0], fgl[core, 0] = split(raw[2 * core])
    square(0, 3)

    loads[8].wait()
    loads[9].wait()
    row = retention[pl.ds(chan, 1), :]
    index = lax.broadcasted_iota(jnp.int32, (total, 1), 0)
    plane, rest = index % nz, index // nz
    wanted = plane * span + (rest % nx) * steps + rest // nx
    there = lax.broadcasted_iota(jnp.int32, (total, total), 1)
    column = jnp.sum(jnp.where(there == wanted, row, 0.0), axis=1, keepdims=True)

    def rows_of(t):
        start = ((t % steps) * nx + t // steps) * nz
        return slice(start, start + nz)

    running = column[:nz]
    rho[:nz] = running
    for t in range(1, span):
        running = running * column[rows_of(t)]
        rho[rows_of(t)] = running
    block_row = lax.broadcasted_iota(jnp.int32, (nz, 1), 0)
    chain = jnp.where(block_row >= 1, shifted(running, 1), 0.0)
    block_factors = [chain]
    for level in range(1, z_bits):
        chain = chain * shifted(chain, 1 << (level - 1))
        block_factors.append(jnp.where(block_row >= (1 << level), chain, 0.0))
    step_row = lax.broadcasted_iota(jnp.int32, (span, 1), 0)
    here = lax.broadcasted_iota(jnp.int32, (span, total), 0)
    there = lax.broadcasted_iota(jnp.int32, (span, total), 1)
    own = jnp.sum(jnp.where(there == here + z * span, row, 0.0), axis=1, keepdims=True)
    own_factors = [jnp.where(step_row >= 1, own, 0.0)]
    for level in range(1, local_bits):
        own = own * shifted(own, 1 << (level - 1))
        own_factors.append(jnp.where(step_row >= (1 << level), own, 0.0))


    landed(sums)
    driving = part_in[0]
    for i in range(1, nc):
        driving = driving + part_in[i]
    drive[x] = driving
    spread = []
    for i in far_first(nx):
        copy = remote(drive.at[x], drive.at[x], x_send.at[i], x_recv.at[i], x_peer(i))
        copy.start()
        spread.append(copy)

    if rounds:
        widened(0)
    if len(rounds) > 1:
        widen(1)
    square(3, 4)
    fgh[1 - core, 0], fgl[1 - core, 0] = split(raw[2 * (1 - core)])
    loads[7].wait()
    th, tl = split(raw[3])
    eye = lax.broadcasted_iota(jnp.int32, (width, width), 0) == lax.broadcasted_iota(
        jnp.int32, (width, width), 1
    )
    product = dot(th, gh[0]) + (dot(th, gl[0]) + dot(tl, gh[0]))
    wh[...], wl[...] = split(jnp.where(eye, 1.0, 0.0) - product)
    take_powers(0, local_bits - 2)

    landed(spread)
    if len(rounds) > 1:
        widened(1)

    local = drive[...].reshape(span, width)
    for level in range(local_bits):
        if level == local_bits - 1:
            take_powers(local_bits - 2, local_bits - 1)
        moved = shifted(local, 1 << level)
        local = local + own_factors[level] * times(moved, fh[level], fl[level])
    ends[z] = local[span - 1 :]
    fbuf[...] = local.reshape(nx, steps, width)
    across = []
    for i in far_first(nz):
        copy = remote(ends.at[z], ends.at[z], e_send.at[i], e_recv.at[i], z_peer(i))
        copy.start()
        across.append(copy)

    square(4, local_bits + z_bits - 2)

    last_plane = z == nz - 1
    corrected = times(local, wh[...], wl[...])
    corrected = jnp.where(last_plane & (step_row == span - 1), local, corrected)
    cbuf[...] = corrected.reshape(nx, steps, width)
    backward = corrected
    for level in (2, 1, 0):
        backward = backward + times(shifted(backward, -(1 << level)), gh[level], gl[level])
    bbuf[...] = backward.reshape(nx, steps, width)
    for level in range(local_bits - 1, 2, -1):
        backward = backward + times(shifted(backward, -(1 << level)), gh[level], gl[level])
    starts[z] = backward[:1]
    for i in far_first(nz):
        copy = remote(starts.at[z], starts.at[z], b_send.at[i], b_recv.at[i], z_peer(i))
        copy.start()
        across.append(copy)

    square(local_bits + z_bits - 2, local_bits + z_bits - 1)
    take_powers(local_bits - 1, local_bits + z_bits - 2)

    landed(across[: nz - 1])

    carry = jnp.where(block_row == 0, prior[...], shifted(ends[...].reshape(nz, width), 1))
    for level in range(z_bits):
        if level == z_bits - 1:
            take_powers(local_bits + z_bits - 2, local_bits + z_bits - 1)
        moved = shifted(carry, 1 << level)
        high, low = fh[local_bits + level], fl[local_bits + level]
        carry = carry + block_factors[level] * times(moved, high, low)

    rows_y[:nz] = times(carry, fh[0], fl[0])
    count = nz
    for level in (*range(3, local_bits), 0, 1, 2):
        rows_y[count : 2 * count] = times(rows_y[:count], fh[level], fl[level])
        count = 2 * count
    rows_y[...] = rows_y[...] * rho[...]

    def own_rows(rows):
        return jnp.concatenate([rows[pl.ds((p * nx + x) * nz + z, 1), :] for p in range(steps)], 0)

    def send_out(state, out, into, send, recv):
        copies = []
        for k in range(width // BLOCK):
            out[k] = state[:, k * BLOCK : (k + 1) * BLOCK]
        for i in far_first(nc):
            there = lax.rem(chan + i, nc)
            copy = remote(out.at[there // 2], into.at[chan], send.at[i], recv.at[i], chan_peer(i))
            copy.start()
            copies.append(copy)
        into[chan] = out[chan // 2]
        return copies


    scaled = rows_y[...].astype(bf16)
    rows_c[...] = dot(scaled, wh[...]) + dot(scaled, wl[...])
    rows_c[total - 1 :] = rows_y[total - 1 :]
    own_corrected = cbuf[x] + own_rows(rows_c)

    for level in (2, 1, 0):
        half = nx * nz << level
        upper = rows_c[half : 2 * half]
        if half >= 256:
            upper = upper.astype(bf16)
            rows_c[:half] = rows_c[:half] + (dot(upper, gh[level]) + dot(upper, gl[level]))
        else:
            rows_c[:half] = rows_c[:half] + times(upper, gh[level], gl[level])

    copies_f = send_out(fbuf[x] + own_rows(rows_y), out_f, in_f, of_send, of_recv)
    landed(across[nz - 1 :])
    whole = block_row == z
    for q in range(nx):
        own_start = bbuf[q][:1]
        if q == 0:
            extra = jnp.where(whole, own_start, starts[...].reshape(nz, width))
        else:
            extra = jnp.where(whole, own_start, 0.0)
        value = rows_c[q * nz : (q + 1) * nz] + extra
        rows_y[q * nz : (q + 1) * nz] = value
        later = jnp.where(block_row < nz - 1, shifted(value, -1), 0.0)
        rows_y[(nx + q) * nz : (nx + q + 1) * nz] = later
    first = pl.multiple_of((1 + x) * nz, nz)
    tail = rows_y[pl.ds(first, nx * nz), :]
    for level in range(local_bits - 1, 2, -1):
        half = nz << (level - 3)
        tail = tail[:half] + times(tail[half:], gh[level], gl[level])
    for level in range(z_bits):
        distance = 1 << level
        moved = jnp.where(block_row < nz - distance, shifted(tail, -distance), 0.0)
        high, low = gh[local_bits + level], gl[local_bits + level]
        tail = tail + times(moved, high, low)
    after = jnp.sum(jnp.where(whole, tail, 0.0), axis=0, keepdims=True)

    row8 = lax.broadcasted_iota(jnp.int32, (steps, 1), 0)
    placed = jnp.where(row8 == steps - 1, after, 0.0)
    state = own_corrected + times(placed, gh[0], gl[0])
    for level in range(3):
        distance = 1 << level
        moved = jnp.where(row8 < steps - distance, shifted(state, -distance), 0.0)
        state = state + times(moved, gh[level], gl[level])
    copies_s = send_out(state, out_s, in_s, os_send, os_recv)

    for copy in sent + copies_f + copies_s:
        copy.wait_send()
    for i in range(local_bits + z_bits - 1):
        power_copy(i).wait_send()
    for copies, into, result in ((copies_f, in_f, filtered), (copies_s, in_s, smoothed)):
        landed(copies)
        result[...] = into[...]


def build(mesh, nx):
    nc = mesh.shape["chan"]
    nz = mesh.shape["tm"] // nx

    def per_device(
        observations, obs_matrix, block_pattern, noise_precision, retention, prior_mean,
        filter_matrix, filter_gain, transition, smoother_gain,
    ):
        series, steps, channels = observations.shape
        width = obs_matrix.shape[1]
        span = nx * steps
        total = span * nz
        powers = total.bit_length() - 1
        vmem = pl.BlockSpec(memory_space=pltpu.VMEM)
        hbm = pl.BlockSpec(memory_space=pl.ANY)
        dma = pltpu.SemaphoreType.DMA
        square = (width, width)
        blocks = width // BLOCK
        result = jax.ShapeDtypeStruct((series, steps, BLOCK), f32)
        both = pl.pallas_call(
            functools.partial(kernel, nx, nz, nc, steps, width, channels),
            out_shape=(result, result),
            in_specs=[hbm] * 10,
            out_specs=(vmem, vmem),
            scratch_shapes=[
                pltpu.VMEM((series, steps, channels), bf16),
                pltpu.VMEM((channels, width), bf16),
                pltpu.SMEM((channels // BLOCK, width // BLOCK), jnp.int32),
                pltpu.VMEM((1, channels), f32),
                pltpu.VMEM((series, total), f32),
                pltpu.VMEM((1, width), f32),
                pltpu.VMEM((4, *square), f32),
                pltpu.VMEM((2, powers, *square), bf16),
                pltpu.VMEM((2, powers, *square), bf16),
                pltpu.VMEM(square, bf16),
                pltpu.VMEM(square, bf16),
                pltpu.VMEM((powers - 1, *square), f32),
                pltpu.VMEM((powers - 1, *square), f32),
                pltpu.VMEM((nc, steps, width), f32),
                pltpu.VMEM((nc, steps, width), f32),
                pltpu.VMEM((nx, steps, width), f32),
                pltpu.VMEM((nz, 1, width), f32),
                pltpu.VMEM((nz, 1, width), f32),
                pltpu.VMEM((total, 1), f32),
                pltpu.VMEM((total, width), f32),
                pltpu.VMEM((total, width), f32),
                pltpu.VMEM((nx, steps, width), f32),
                pltpu.VMEM((nx, steps, width), f32),
                pltpu.VMEM((nx, steps, width), f32),
                pltpu.VMEM((blocks, steps, BLOCK), f32),
                pltpu.VMEM((blocks, steps, BLOCK), f32),
                pltpu.VMEM((nc, steps, BLOCK), f32),
                pltpu.VMEM((nc, steps, BLOCK), f32),
                dma((10,)),
                dma((nc,)), dma((nc,)),
                dma((nx,)), dma((nx,)),
                dma((nz,)), dma((nz,)),
                dma((nz,)), dma((nz,)),
                dma((nc,)), dma((nc,)),
                dma((nc,)), dma((nc,)),
                dma((powers,)), dma((powers,)),
                pltpu.SemaphoreType.REGULAR((2,)),
            ],
            compiler_params=pltpu.CompilerParams(
                collective_id=0, has_side_effects=True, vmem_limit_bytes=LIMIT
            ),
        )(
            observations, obs_matrix, block_pattern, noise_precision.reshape(1, channels),
            retention, prior_mean.reshape(1, width),
            filter_matrix, filter_gain, transition, smoother_gain,
        )
        odd = lax.rem(lax.axis_index("chan"), 2) == 1
        half = BLOCK // 2
        return tuple(jnp.where(odd, array[:, :, half:], array[:, :, :half]) for array in both)

    placed = (
        P(None, "tm", "chan"), P("chan", None), P("chan", None), P("chan"),
        P(), P(), P(), P(), P(), P(),
    )
    return jax.shard_map(
        per_device,
        mesh=mesh,
        in_specs=placed,
        out_specs=(P(None, "tm", "chan"), P(None, "tm", "chan")),
        check_vma=False,
    )


def solution(mesh):
    return build(mesh, PLANE)
```
